256 devices in a mesh: samp: 32 (over x, z), prot: 8 (over y, core).
Axes of the slice: x: 4, y: 4, z: 8, core: 2. Of those that a mesh axis runs over, the one named last changes fastest.
Arguments:
- bin_ids: int32 [736, 131072], P('prot', 'samp'), may hold values from 0 to 1023
- plate_ids: int32 [131072], P('samp'), may hold values from 0 to 23, as said below
- covariates: float32 [40, 131072], P(None, 'samp'), may hold values from -50 to 50
- dosages: bfloat16 [1024, 131072], P(None, 'samp'), may hold values from 0 to 2
Outputs:
- t_stats: float32 [1024, 736], P('samp', 'prot')
The draws below stay inside these ranges and needn't reach their ends.
Inputs may be any that keep to these rules, and one draw needn't show every extreme that they name: `plate_ids`: every plate holds at least one sample.
All inputs are finite; a program needn't handle non-finite values.
Results may differ from the reference program's by a relative error of at most 0.0003.
Values sent between devices are 32-bit elements; how exact they have to be, the bound alone decides.
No kernel may reach another device: no remote copies, remote signals or barrier semaphores. Data moves between devices by JAX's collectives and lax.ppermute only.
A program may use at most 128 MiB of HBM per device.

```python
import math
import jax
import jax.numpy as jnp
from jax import lax

PROTEINS = 736
BINS = 1024
COVARS = 40
PLATES = 24
VARIANTS = 1024
SAMPLES = 131072
DESIGN = 64


def shared_plates(key):
    plate_key = jax.random.fold_in(key, 101)
    plate_draw = jax.random.randint(plate_key, (SAMPLES,), 0, PLATES, dtype=jnp.int32)
    position = jnp.arange(SAMPLES, dtype=jnp.int32)
    return jnp.where(position < PLATES, position, plate_draw).astype(jnp.int32)


def shared_factors(key):
    factor_key = jax.random.fold_in(key, 202)
    return jnp.clip(jax.random.normal(factor_key, (COVARS, SAMPLES), jnp.float32), -5.0, 5.0)


def draw_plate_ids(key, part):
    return shared_plates(key)


def draw_bin_ids(key, part):
    plates = shared_plates(key)
    key = jax.random.fold_in(key, 3)
    shift_key, noise_key, limit_key, share_key, flag_key = jax.random.split(key, 5)
    shift_table = jax.random.randint(shift_key, (PROTEINS, PLATES), 0, BINS // 2, dtype=jnp.int32)
    noise_part = jax.random.randint(noise_key, (PROTEINS, SAMPLES), 0, BINS // 4 + 1, dtype=jnp.int32)
    position = jnp.arange(SAMPLES, dtype=jnp.int32)
    drift_part = position * (BINS // 4) // SAMPLES
    plate_shift = jnp.take(shift_table, plates, axis=1)
    bin_draw = noise_part + drift_part[None, :] + plate_shift
    row_index = jnp.arange(PROTEINS, dtype=jnp.int32)[:, None]
    col_index = position[None, :]
    limit_bin = jax.random.randint(limit_key, (PROTEINS, 1), 0, BINS // 2, dtype=jnp.int32)
    censor_share = jax.random.randint(share_key, (PROTEINS, 1), 400, 922, dtype=jnp.int32)
    censor_share = jnp.where(row_index == 0, 921, censor_share)
    censor_flag = jax.random.randint(flag_key, (PROTEINS, SAMPLES), 0, 1024, dtype=jnp.int32) < censor_share
    bin_draw = jnp.where(censor_flag, limit_bin, bin_draw)
    bin_draw = jnp.where((row_index == 0) & (col_index == 0), 0, bin_draw)
    bin_draw = jnp.where((row_index == 0) & (col_index == SAMPLES - 1), BINS - 1, bin_draw)
    return bin_draw.astype(jnp.int32)


def draw_covariates(key, part):
    factors = shared_factors(key)
    key = jax.random.fold_in(key, 5)
    column_scale = jax.random.uniform(key, (COVARS, 1), jnp.float32, 0.5, 2.0)
    return factors * column_scale


def draw_dosages(key, part):
    factors = shared_factors(key)
    plates = shared_plates(key)
    key = jax.random.fold_in(key, 7)
    weight_key, noise_key, offset_key, batch_key = jax.random.split(key, 4)
    weights = 0.2 * jax.random.normal(weight_key, (VARIANTS, COVARS), jnp.float32)
    batch_table = 0.5 * jax.random.normal(batch_key, (VARIANTS, PLATES), jnp.float32)
    noise_part = jax.random.normal(noise_key, (VARIANTS, SAMPLES), jnp.float32)
    offset = jax.random.normal(offset_key, (VARIANTS, 1), jnp.float32)
    logit_value = offset + noise_part + jnp.take(batch_table, plates, axis=1)
    for column in range(COVARS):
        logit_value = logit_value + weights[:, column:column + 1] * factors[column:column + 1, :]
    return (2.0 * jax.nn.sigmoid(logit_value)).astype(jnp.bfloat16)


def setup_inputs(seed: int = 0) -> dict:
    seeds = jax.random.split(jax.random.key(seed), 5)
    bin_ids = draw_bin_ids(jax.random.fold_in(seeds[4], 71), 0)
    plate_ids = draw_plate_ids(jax.random.fold_in(seeds[4], 71), 0)
    covariates = draw_covariates(jax.random.fold_in(seeds[4], 71), 0)
    dosages = draw_dosages(jax.random.fold_in(seeds[4], 71), 0)
    return dict(bin_ids=bin_ids, plate_ids=plate_ids, covariates=covariates, dosages=dosages)


exact_mode = lax.Precision.HIGHEST
tiny_eps = 1e-06

def normal_quantile(level):
    return math.sqrt(2.0) * lax.erf_inv(2.0 * level - 1.0)

def reference(bin_ids, plate_ids, covariates, dosages):
    sample_total = bin_ids.shape[1]
    row_index = jnp.arange(PROTEINS, dtype=jnp.int32)[:, None]
    counts = jnp.zeros((PROTEINS, BINS), jnp.float32).at[row_index, bin_ids].add(1.0)
    preceding = jnp.cumsum(counts, axis=1) - counts
    middle = preceding + 0.5 * (counts + 1.0)
    rank_values = normal_quantile((middle - 0.375) / (sample_total + 0.25))
    expressed = jnp.take_along_axis(rank_values, bin_ids, axis=1)
    plate_rows = (plate_ids[None, :] == jnp.arange(PLATES, dtype=jnp.int32)[:, None]).astype(jnp.float32)
    design = jnp.concatenate([covariates, plate_rows], axis=0)
    dose_float = dosages.astype(jnp.float32)
    gram_sum = jnp.dot(design.astype(jnp.float32), design.T.astype(jnp.float32), precision=exact_mode, preferred_element_type=jnp.float32)
    chol_factor = jnp.linalg.cholesky(gram_sum)
    dose_proj = jnp.dot(design.astype(jnp.float32), dose_float.T.astype(jnp.float32), precision=exact_mode, preferred_element_type=jnp.float32)
    expr_proj = jnp.dot(design.astype(jnp.float32), expressed.T.astype(jnp.float32), precision=exact_mode, preferred_element_type=jnp.float32)
    dose_load = jax.scipy.linalg.cho_solve((chol_factor, True), dose_proj)
    prot_load = jax.scipy.linalg.cho_solve((chol_factor, True), expr_proj)
    dose_resid = dose_float - jnp.dot(dose_load.T.astype(jnp.float32), design.astype(jnp.float32), precision=exact_mode, preferred_element_type=jnp.float32)
    expr_resid = expressed - jnp.dot(prot_load.T.astype(jnp.float32), design.astype(jnp.float32), precision=exact_mode, preferred_element_type=jnp.float32)
    cross = jnp.dot(dose_resid.astype(jnp.float32), expr_resid.T.astype(jnp.float32), precision=exact_mode, preferred_element_type=jnp.float32)
    dose_norm = lax.optimization_barrier(jnp.sum(dose_resid * dose_resid, axis=1))
    expr_norm = lax.optimization_barrier(jnp.sum(expr_resid * expr_resid, axis=1))
    corr = cross * lax.rsqrt(dose_norm[:, None] * expr_norm[None, :] + tiny_eps)
    freedom = sample_total - DESIGN - 1.0
    return corr * jnp.sqrt(freedom / (1.0 - corr * corr))
```

```python
import functools
import math

import jax
import jax.numpy as jnp
from jax import lax
from jax.experimental import pallas as pl
from jax.experimental.pallas import tpu as pltpu
from jax.sharding import PartitionSpec as P

BINS = 1024
PLATES = 24
COVARS = 40
DESIGN = 64
LANES = 128
tiny_eps = 1e-06
F32 = jnp.float32
BF16 = jnp.bfloat16
exact_mode = lax.Precision.HIGHEST
NT = (((1,), (1,)), ((), ()))
NN = (((1,), (0,)), ((), ()))


def vmem_params(mib):
    return pltpu.CompilerParams(vmem_limit_bytes=mib * 1024 * 1024)


def lane_ids(shape):
    return lax.broadcasted_iota(jnp.int32, shape, len(shape) - 1)


def design_parts(cov, plates):
    width = cov.shape[1]
    rows = lax.broadcasted_iota(jnp.int32, (PLATES, width), 0)
    plate_rows = jnp.where(plates == rows, 1.0, 0.0).astype(F32)
    design = jnp.concatenate([cov, plate_rows], axis=0)
    high = design.astype(BF16)
    rest = design - high.astype(F32)
    middle = rest.astype(BF16)
    low = (rest - middle.astype(F32)).astype(BF16)
    return high, middle, low


def fold_lanes(wide):
    first, second = wide[:, :LANES], wide[:, LANES:]
    pair = first + second
    return pair + pltpu.roll(pair, 64, 1)


def hist_kernel(bins_ref, cov_ref, plate_ref, out_ref, table_ref):
    step = pl.program_id(0)
    width = bins_ref.shape[1]
    chunk = 1024
    ids32 = lax.broadcasted_iota(jnp.int32, (32, chunk), 0)
    total = jnp.zeros((256, 256), F32)
    for start in range(0, width, chunk):
        bins = bins_ref[:, start : start + chunk]
        upper, lower = bins >> 5, bins & 31
        left = jnp.concatenate(
            [jnp.where(upper[p : p + 1] == ids32, 1.0, 0.0).astype(BF16) for p in range(8)], axis=0
        )
        right = jnp.concatenate(
            [jnp.where(lower[p : p + 1] == ids32, 1.0, 0.0).astype(BF16) for p in range(8)], axis=0
        )
        total = total + lax.dot_general(left, right, NT, preferred_element_type=F32)
    lane = lane_ids((32, 256)) // 32
    diag = jnp.zeros((32, 256), F32)
    for p in range(8):
        diag = jnp.where(lane == p, total[32 * p : 32 * p + 32], diag)
    table_ref[...] = diag[:, :LANES]
    table_ref2 = table_ref
    block = lane_ids((8, LANES)) // 32
    for half in range(2):
        table_ref2[...] = diag[:, half * LANES : (half + 1) * LANES]
        rows = [table_ref2[pl.ds(c, 8, stride=4), :] for c in range(4)]
        for q in range(4):
            out = jnp.zeros((8, LANES), F32)
            for c in range(4):
                shift = ((c - q) % 4) * 32
                moved = pltpu.roll(rows[c], shift, 1) if shift else rows[c]
                out = jnp.where(block == c, moved, out)
            p = half * 4 + q
            out_ref[8 * p : 8 * p + 8, :] = out

    @pl.when(step == pl.num_programs(0) - 1)
    def _():
        high, middle, low = design_parts(cov_ref[...], plate_ref[...])
        stack = jnp.concatenate([high, middle, low, jnp.zeros_like(high)], axis=0)
        wide = lax.dot_general(stack[:192], stack, NT, preferred_element_type=F32)
        gram = fold_lanes(wide[:64] + wide[64:128] + wide[128:192])
        out_ref[32:64, :] = jnp.where(lane_ids((32, LANES)) < 64, gram[:32], gram[32:])


def histogram(bin_ids, covariates, plates):
    width = bin_ids.shape[1]
    return pl.pallas_call(
        hist_kernel,
        grid=(12,),
        in_specs=[
            pl.BlockSpec((8, width), lambda g: (g, 0)),
            pl.BlockSpec((COVARS, width), lambda g: (0, 0)),
            pl.BlockSpec((1, width), lambda g: (0, 0)),
        ],
        out_specs=pl.BlockSpec((64, LANES), lambda g: (g, 0)),
        out_shape=jax.ShapeDtypeStruct((768, LANES), F32),
        scratch_shapes=[pltpu.VMEM((32, LANES), F32)],
        compiler_params=vmem_params(48),
        name="histogram",
    )(bin_ids, covariates, plates)


def dose_kernel(dose_ref, cov_ref, plate_ref, proj_ref, square_ref, total_ref):
    step = pl.program_id(0)
    high, middle, low = design_parts(cov_ref[...], plate_ref[...])
    stack = jnp.concatenate([high, middle, low, jnp.zeros_like(high)], axis=0)
    dose = dose_ref[...]
    term = lax.dot_general(dose, stack, NT, preferred_element_type=F32)
    wide = dose.astype(F32)
    wide = wide * wide
    part = wide[:, :LANES]
    for start in range(LANES, wide.shape[1], LANES):
        part = part + wide[:, start : start + LANES]

    @pl.when(step == 0)
    def _():
        total_ref[...] = term
        square_ref[...] = part

    @pl.when(step > 0)
    def _():
        total_ref[...] += term
        square_ref[...] += part

    @pl.when(step == pl.num_programs(0) - 1)
    def _():
        half = lane_ids((16, LANES)) < 64
        for c in range(32):
            both = fold_lanes(total_ref[32 * c : 32 * c + 32, :])
            proj_ref[16 * c : 16 * c + 16, :] = jnp.where(half, both[:16], both[16:])


def dose_products(dosages, covariates, plates):
    count, width = dosages.shape
    tile = 512
    return pl.pallas_call(
        dose_kernel,
        grid=(width // tile,),
        in_specs=[
            pl.BlockSpec((count, tile), lambda s: (0, s)),
            pl.BlockSpec((COVARS, tile), lambda s: (0, s)),
            pl.BlockSpec((1, tile), lambda s: (0, s)),
        ],
        out_specs=[
            pl.BlockSpec((count // 2, LANES), lambda s: (0, 0)),
            pl.BlockSpec((count, LANES), lambda s: (0, 0)),
        ],
        out_shape=[
            jax.ShapeDtypeStruct((count // 2, LANES), F32),
            jax.ShapeDtypeStruct((count, LANES), F32),
        ],
        scratch_shapes=[pltpu.VMEM((count, 256), F32)],
        compiler_params=vmem_params(32),
        cost_estimate=pl.CostEstimate(
            flops=2 * count * width * 256, bytes_accessed=count * width * 2, transcendentals=0
        ),
        name="dose_products",
    )(dosages, covariates, plates)


def erf_inverse(x):
    w = -jnp.log1p(-x * x)
    small = w < 5.0
    shifted = jnp.where(small, w - 2.5, jnp.sqrt(w) - 3.0)
    near = (
        2.81022636e-08, 3.43273939e-07, -3.5233877e-06, -4.39150654e-06, 0.00021858087,
        -0.00125372503, -0.00417768164, 0.246640727, 1.50140941,
    )
    far = (
        -0.000200214257, 0.000100950558, 0.00134934322, -0.00367342844, 0.00573950773,
        -0.0076224613, 0.00943887047, 1.00167406, 2.83297682,
    )
    value = jnp.where(small, near[0], far[0])
    for a, b in zip(near[1:], far[1:]):
        value = value * shifted + jnp.where(small, a, b)
    return value * x


def table_kernel(sample_total, base_ref, parts_ref, out_ref):
    counts = jnp.sum(parts_ref[...], axis=0)
    rows = counts.shape[0]
    row = lax.broadcasted_iota(jnp.int32, (LANES, LANES), 0)
    before = (row < lane_ids((LANES, LANES))).astype(F32)
    inside = lax.dot_general(
        counts, before, NN, precision=exact_mode, preferred_element_type=F32
    )
    totals = jnp.broadcast_to(jnp.sum(counts, axis=1, keepdims=True), counts.shape)
    row = lax.broadcasted_iota(jnp.int32, (rows, rows), 0)
    col = lane_ids((rows, rows))
    earlier = ((col < row) & (col // 8 == row // 8)).astype(F32)
    outside = lax.dot_general(
        earlier, totals, NN, precision=exact_mode, preferred_element_type=F32
    )
    middle = inside + outside + 0.5 * (counts + 1.0)
    level = (middle - 0.375) / (sample_total + 0.25)
    values = math.sqrt(2.0) * erf_inverse(2.0 * level - 1.0)
    place = base_ref[0] + lax.broadcasted_iota(jnp.int32, counts.shape, 0)
    values = jnp.where(place < 736, values, counts)
    for n in range(out_ref.shape[0]):
        out_ref[n] = values


def rank_table(parts, sample_total, base):
    return pl.pallas_call(
        functools.partial(table_kernel, float(sample_total)),
        in_specs=[
            pl.BlockSpec(memory_space=pltpu.SMEM),
            pl.BlockSpec(memory_space=pltpu.VMEM),
        ],
        out_specs=pl.BlockSpec(memory_space=pltpu.VMEM),
        out_shape=jax.ShapeDtypeStruct(parts.shape, F32),
        compiler_params=vmem_params(16),
        name="rank_table",
    )(base, parts)


def cross_kernel(
    bins_ref, table_ref, dose_ref, cov_ref, plate_ref, dproj_ref, dsq_ref,
    out_ref, level_ref, total_ref, design_ref, square_ref,
):
    step = pl.program_id(0)
    tile = bins_ref.shape[1]

    @pl.when(step == 0)
    def _():
        level_ref[...] = jnp.zeros_like(level_ref)
        total_ref[...] = jnp.zeros_like(total_ref)
        design_ref[...] = jnp.zeros_like(design_ref)
        square_ref[...] = jnp.zeros_like(square_ref)

    for g in range(0, 12, 2):
        highs, lows = [[], []], [[], []]
        for half in range(2):
            first = g + half
            tables = [table_ref[pl.ds(64 * first + k, 8, stride=8), :] for k in range(8)]
            pieces = []
            for start in range(0, tile, LANES):
                bins = bins_ref[8 * first : 8 * first + 8, start : start + LANES]
                lower, upper = bins & 127, bins >> 7
                value = jnp.take_along_axis(tables[0], lower, axis=1, mode="promise_in_bounds")
                for k in range(1, 8):
                    other = jnp.take_along_axis(tables[k], lower, axis=1, mode="promise_in_bounds")
                    value = jnp.where(upper == k, other, value)
                if first == 11:
                    keep = lax.broadcasted_iota(jnp.int32, (8, LANES), 0) < 4
                    value = jnp.where(keep, value, 0.0)
                pieces.append(value)
            squares = pieces[0] * pieces[0]
            for piece in pieces[1:]:
                squares = squares + piece * piece
            square_ref[8 * first : 8 * first + 8, :] += squares
            highs[half] = jnp.concatenate(pieces, axis=1)
        value = jnp.concatenate(highs, axis=0)
        high = value.astype(BF16)
        low = (value - high.astype(F32)).astype(BF16)
        level_ref[8 * g : 8 * g + 16, :] = high
        level_ref[128 + 8 * g : 128 + 8 * g + 16, :] = low
    level = level_ref[...]
    total_ref[...] += lax.dot_general(dose_ref[...], level, NT, preferred_element_type=F32)
    stack = jnp.concatenate(design_parts(cov_ref[...], plate_ref[...]), axis=0)
    design_ref[...] += lax.dot_general(stack, level, NT, preferred_element_type=F32)

    @pl.when(step == pl.num_programs(0) - 1)
    def _():
        wide = design_ref[0:64, :] + design_ref[64:128, :] + design_ref[128:192, :]
        proj = wide[:, :LANES] + wide[:, LANES:]
        squares = lax.dot_general(
            jnp.ones((8, LANES), F32), square_ref[...], NT,
            precision=exact_mode, preferred_element_type=F32,
        )
        lane = lane_ids((256, LANES))
        for x in range(4):
            rows = slice(256 * x, 256 * x + 256)
            cross = total_ref[rows, :LANES] + total_ref[rows, LANES:]
            dose_sq = jnp.sum(dsq_ref[rows, :], axis=1, keepdims=True)
            out_ref[x, 0:256, :] = jnp.where(lane == 96, dose_sq, cross)
            out_ref[x, 256:384, :] = dproj_ref[128 * x : 128 * x + 128, :]
            out_ref[x, 384:448, :] = proj
            out_ref[x, 448:456, :] = squares


def cross_products(bin_ids, table, dosages, covariates, plates, dose_proj, dose_sq):
    count, width = dosages.shape
    tile = 512
    whole = pl.BlockSpec(memory_space=pltpu.VMEM)
    return pl.pallas_call(
        cross_kernel,
        grid=(width // tile,),
        in_specs=[
            pl.BlockSpec((96, tile), lambda s: (0, s)),
            whole,
            pl.BlockSpec((count, tile), lambda s: (0, s)),
            pl.BlockSpec((COVARS, tile), lambda s: (0, s)),
            pl.BlockSpec((1, tile), lambda s: (0, s)),
            whole,
            whole,
        ],
        out_specs=whole,
        out_shape=jax.ShapeDtypeStruct((4, 456, LANES), F32),
        scratch_shapes=[
            pltpu.VMEM((256, tile), BF16),
            pltpu.VMEM((count, 256), F32),
            pltpu.VMEM((192, 256), F32),
            pltpu.VMEM((LANES, LANES), F32),
        ],
        compiler_params=vmem_params(32),
        name="cross_products",
    )(bin_ids, table, dosages, covariates, plates, dose_proj, dose_sq)


def regroup_kernel(parts_ref, out_ref):
    total = parts_ref[0] + parts_ref[1] + parts_ref[2] + parts_ref[3]
    for z in range(8):
        out_ref[z, 0:32, :] = total[32 * z : 32 * z + 32]
        out_ref[z, 32:48, :] = total[256 + 16 * z : 256 + 16 * z + 16]
        out_ref[z, 48:120, :] = total[384:456]


def regroup(parts):
    whole = pl.BlockSpec(memory_space=pltpu.VMEM)
    return pl.pallas_call(
        regroup_kernel,
        in_specs=[whole],
        out_specs=whole,
        out_shape=jax.ShapeDtypeStruct((8, 120, LANES), F32),
        compiler_params=vmem_params(16),
        name="regroup",
    )(parts)


def finish_kernel(freedom, parts_ref, inverse_ref, out_ref):
    total = parts_ref[0]
    for z in range(1, 8):
        total = total + parts_ref[z]
    cross, dose, proj, squares = total[0:32], total[32:48], total[48:112], total[112:113]
    inverse = inverse_ref[...]
    dot = functools.partial(
        lax.dot_general, precision=exact_mode, preferred_element_type=F32
    )
    expr_white = dot(inverse, proj, NN)
    dose_both = jnp.concatenate([dose[:, :64], dose[:, 64:]], axis=0)
    dose_white = dot(dose_both, inverse, NT)
    expr_norm = squares - jnp.sum(expr_white * expr_white, axis=0, keepdims=True)
    dose_norm = cross[:, 96:97] - jnp.sum(dose_white * dose_white, axis=1, keepdims=True)
    cross = cross - dot(dose_white, expr_white, NN)
    corr = cross * lax.rsqrt(dose_norm * expr_norm + tiny_eps)
    stats = corr * jnp.sqrt(freedom / (1.0 - corr * corr))
    out_ref[...] = stats[:, : out_ref.shape[1]]


def finish(parts, inverse, freedom, proteins):
    whole = pl.BlockSpec(memory_space=pltpu.VMEM)
    return pl.pallas_call(
        functools.partial(finish_kernel, float(freedom)),
        in_specs=[whole, whole],
        out_specs=whole,
        out_shape=jax.ShapeDtypeStruct((32, proteins), F32),
        compiler_params=vmem_params(16),
        name="finish",
    )(parts, inverse)


def body(bin_ids, plate_ids, covariates, dosages):
    sample_total = bin_ids.shape[1] * lax.axis_size("samp")
    plates = plate_ids[None, :]
    x_groups = [[x * 8 + z for x in range(4)] for z in range(8)]
    z_groups = [[x * 8 + z for z in range(8)] for x in range(4)]
    base = (lax.axis_index("samp") * 24).astype(jnp.int32)[None]

    counts = histogram(bin_ids, covariates, plates).reshape(32, 24, LANES)
    counts = lax.all_to_all(counts, "samp", 0, 0, tiled=True)
    dose_proj, dose_sq = dose_products(dosages, covariates, plates)
    table = rank_table(counts, sample_total, base)
    table = lax.all_to_all(table, "samp", 0, 0, tiled=True).reshape(768, LANES)
    parts = cross_products(bin_ids, table, dosages, covariates, plates, dose_proj, dose_sq)
    gram = jnp.concatenate([table[736:, :64], table[736:, 64:]], axis=0)
    factor = lax.linalg.cholesky(gram, symmetrize_input=False)
    inverse = lax.linalg.triangular_solve(
        factor, jnp.eye(DESIGN, dtype=F32), left_side=True, lower=True
    )
    parts = lax.all_to_all(parts, "samp", 0, 0, axis_index_groups=x_groups, tiled=True)
    parts = regroup(parts)
    parts = lax.all_to_all(parts, "samp", 0, 0, axis_index_groups=z_groups, tiled=True)
    return finish(parts, inverse, sample_total - DESIGN - 1.0, bin_ids.shape[0])


def solution(mesh):
    placed = (P("prot", "samp"), P("samp"), P(None, "samp"), P(None, "samp"))
    return jax.shard_map(
        body, mesh=mesh, in_specs=placed, out_specs=P("samp", "prot"), check_vma=False
    )
```

```python
import functools
import math

import jax
import jax.numpy as jnp
from jax import lax
from jax.experimental import pallas as pl
from jax.experimental.pallas import tpu as pltpu
from jax.sharding import PartitionSpec as P

BINS = 1024
PLATES = 24
COVARS = 40
DESIGN = 64
DOSE_CHUNK = 1024
CROSS_CHUNK = 1024
LANES = 128
tiny_eps = 1e-06
F32 = jnp.float32
BF16 = jnp.bfloat16
FP8 = jnp.float8_e4m3fn
exact_mode = lax.Precision.HIGHEST
NT = (((1,), (1,)), ((), ()))
NN = (((1,), (0,)), ((), ()))


def vmem_params(mib):
    return pltpu.CompilerParams(vmem_limit_bytes=mib * 1024 * 1024)


def lane_ids(shape):
    return lax.broadcasted_iota(jnp.int32, shape, len(shape) - 1)


def design_parts(cov, plates):
    width = cov.shape[1]
    rows = lax.broadcasted_iota(jnp.int32, (PLATES, width), 0)
    plate_rows = jnp.where(plates == rows, 1.0, 0.0).astype(F32)
    design = jnp.concatenate([cov, plate_rows], axis=0)
    high = design.astype(BF16)
    rest = design - high.astype(F32)
    middle = rest.astype(BF16)
    low = (rest - middle.astype(F32)).astype(BF16)
    return high, middle, low


def fold_lanes(wide):
    first, second = wide[:, :LANES], wide[:, LANES:]
    pair = first + second
    return pair + pltpu.roll(pair, 64, 1)


WAITS = {0: (0, 1), 2: tuple(range(2, 14))}


def hist_kernel(bins_hbm, cov_hbm, plate_hbm, out_ref, bins_ref, cov_ref, plate_ref, table_ref, sems):
    proteins, width = bins_hbm.shape
    chunk = 1024
    groups = [(start, min(8, proteins - start)) for start in range(0, proteins, 8)]
    copies = [
        pltpu.make_async_copy(
            bins_hbm.at[pl.ds(start, size)], bins_ref.at[pl.ds(start, size)], sems.at[n]
        )
        for n, (start, size) in enumerate(groups)
    ]
    copies.append(pltpu.make_async_copy(cov_hbm, cov_ref, sems.at[len(groups)]))
    copies.append(pltpu.make_async_copy(plate_hbm, plate_ref, sems.at[len(groups) + 1]))
    for copy in copies:
        copy.start()
    ids = lax.broadcasted_iota(jnp.int32, (32, chunk), 0).astype(jnp.int8)
    one = jnp.ones((32, chunk), F32).astype(FP8)
    zero = jnp.zeros((32, chunk), F32).astype(FP8)
    block = lane_ids((8, LANES)) // 32
    for n, (first, size) in enumerate(groups):
        for k in WAITS.get(n, ()):
            copies[k].wait()
        side = 32 * size
        total = jnp.zeros((side, side), F32)
        for start in range(0, width, chunk):
            bins = bins_ref[first : first + size, start : start + chunk]
            left, right = [], []
            for p in range(size):
                row = jnp.broadcast_to(bins[p : p + 1], (32, chunk))
                left.append(jnp.where((row >> 5).astype(jnp.int8) == ids, one, zero))
                right.append(jnp.where((row & 31).astype(jnp.int8) == ids, one, zero))
            total = total + lax.dot_general(
                jnp.concatenate(left, axis=0),
                jnp.concatenate(right, axis=0),
                NT,
                preferred_element_type=F32,
            )
        lane = lane_ids((32, side)) // 32
        diag = total[:32]
        for p in range(1, size):
            diag = jnp.where(lane == p, total[32 * p : 32 * p + 32], diag)
        for half in range(side // LANES):
            table_ref[n % 2, half] = diag[:, half * LANES : (half + 1) * LANES]
            rows = [table_ref[n % 2, half, pl.ds(c, 8, stride=4), :] for c in range(4)]
            for q in range(4):
                out = rows[q]
                for c in range(4):
                    shift = ((c - q) % 4) * 32
                    moved = pltpu.roll(rows[c], shift, 1) if shift else rows[c]
                    out = jnp.where(block == c, moved, out)
                p = first + half * 4 + q
                out_ref[8 * p : 8 * p + 8, :] = out
    high, middle, low = design_parts(cov_ref[...], plate_ref[...])
    stack = jnp.concatenate([high, middle, low, jnp.zeros_like(high)], axis=0)
    wide = lax.dot_general(stack[:192], stack, NT, preferred_element_type=F32)
    gram = fold_lanes(wide[:64] + wide[64:128] + wide[128:192])
    out_ref[8 * proteins :, :] = jnp.where(lane_ids((32, LANES)) < 64, gram[:32], gram[32:])


def histogram(bin_ids, covariates, plates):
    proteins, width = bin_ids.shape
    hbm = pl.BlockSpec(memory_space=pl.ANY)
    return pl.pallas_call(
        hist_kernel,
        in_specs=[hbm, hbm, hbm],
        out_specs=pl.BlockSpec(memory_space=pltpu.VMEM),
        out_shape=jax.ShapeDtypeStruct((768, LANES), F32),
        scratch_shapes=[
            pltpu.VMEM((96, width), jnp.int32),
            pltpu.VMEM((COVARS, width), F32),
            pltpu.VMEM((1, width), jnp.int32),
            pltpu.VMEM((2, 2, 32, LANES), F32),
            pltpu.SemaphoreType.DMA((14,)),
        ],
        compiler_params=vmem_params(60),
        name="histogram",
    )(bin_ids, covariates, plates)


def dose_kernel(dose_hbm, cov_ref, plate_ref, proj_ref, square_ref, dose_ref, total_ref, part_ref, sems):
    chunk = dose_ref.shape[2]
    copies = [
        pltpu.make_async_copy(
            dose_hbm.at[:, pl.ds(c * chunk, chunk)], dose_ref.at[c], sems.at[c]
        )
        for c in range(dose_ref.shape[0])
    ]
    for copy in copies:
        copy.start()
    high, middle, low = design_parts(cov_ref[...], plate_ref[...])
    stack = jnp.concatenate([high, middle, low, jnp.zeros_like(high)], axis=0)
    for c in range(len(copies)):
        copies[c].wait()
        for r in range(0, dose_ref.shape[1], 256):
            dose = dose_ref[c, r : r + 256, :]
            term = lax.dot_general(
                dose, stack[:, c * chunk : (c + 1) * chunk], NT, preferred_element_type=F32
            )
            wide = dose.astype(F32)
            wide = wide * wide
            part = wide[:, :LANES]
            for start in range(LANES, chunk, LANES):
                part = part + wide[:, start : start + LANES]
            if c == 0:
                total_ref[r : r + 256, :] = term
                part_ref[r : r + 256, :] = part
            else:
                total_ref[r : r + 256, :] += term
                part_ref[r : r + 256, :] += part
    half = lane_ids((16, LANES)) < 64
    for c in range(32):
        both = fold_lanes(total_ref[32 * c : 32 * c + 32, :])
        proj_ref[16 * c : 16 * c + 16, :] = jnp.where(half, both[:16], both[16:])
    squares = lax.dot_general(
        jnp.ones((8, LANES), F32), part_ref[...], NT,
        precision=exact_mode, preferred_element_type=F32,
    )
    for c in range(8):
        square_ref[c : c + 1, :] = squares[0:1, LANES * c : LANES * (c + 1)]


def dose_products(dosages, covariates, plates):
    count, width = dosages.shape
    chunk = DOSE_CHUNK
    whole = pl.BlockSpec(memory_space=pltpu.VMEM)
    return pl.pallas_call(
        dose_kernel,
        in_specs=[pl.BlockSpec(memory_space=pl.ANY), whole, whole],
        out_specs=[whole, whole],
        out_shape=[
            jax.ShapeDtypeStruct((count // 2, LANES), F32),
            jax.ShapeDtypeStruct((8, LANES), F32),
        ],
        scratch_shapes=[
            pltpu.VMEM((width // chunk, count, chunk), BF16),
            pltpu.VMEM((count, 256), F32),
            pltpu.VMEM((count, LANES), F32),
            pltpu.SemaphoreType.DMA((width // chunk,)),
        ],
        compiler_params=vmem_params(60),
        cost_estimate=pl.CostEstimate(
            flops=2 * count * width * 256, bytes_accessed=count * width * 2, transcendentals=0
        ),
        name="dose_products",
    )(dosages, covariates, plates)


def erf_inverse(x):
    w = -jnp.log1p(-x * x)
    small = w < 5.0
    shifted = jnp.where(small, w - 2.5, jnp.sqrt(w) - 3.0)
    near = (
        2.81022636e-08, 3.43273939e-07, -3.5233877e-06, -4.39150654e-06, 0.00021858087,
        -0.00125372503, -0.00417768164, 0.246640727, 1.50140941,
    )
    far = (
        -0.000200214257, 0.000100950558, 0.00134934322, -0.00367342844, 0.00573950773,
        -0.0076224613, 0.00943887047, 1.00167406, 2.83297682,
    )
    value = jnp.where(small, near[0], far[0])
    for a, b in zip(near[1:], far[1:]):
        value = value * shifted + jnp.where(small, a, b)
    return value * x


def table_kernel(sample_total, base_ref, parts_ref, out_ref):
    counts = jnp.sum(parts_ref[...], axis=0)
    rows = counts.shape[0]
    row = lax.broadcasted_iota(jnp.int32, (LANES, LANES), 0)
    before = (row < lane_ids((LANES, LANES))).astype(F32)
    inside = lax.dot_general(
        counts, before, NN, precision=exact_mode, preferred_element_type=F32
    )
    totals = jnp.broadcast_to(jnp.sum(counts, axis=1, keepdims=True), counts.shape)
    row = lax.broadcasted_iota(jnp.int32, (rows, rows), 0)
    col = lane_ids((rows, rows))
    earlier = ((col < row) & (col // 8 == row // 8)).astype(F32)
    outside = lax.dot_general(
        earlier, totals, NN, precision=exact_mode, preferred_element_type=F32
    )
    middle = inside + outside + 0.5 * (counts + 1.0)
    level = (middle - 0.375) / (sample_total + 0.25)
    values = math.sqrt(2.0) * erf_inverse(2.0 * level - 1.0)
    place = base_ref[0] + lax.broadcasted_iota(jnp.int32, counts.shape, 0)
    values = jnp.where(place < 736, values, counts)
    for n in range(out_ref.shape[0]):
        out_ref[n] = values


def rank_table(parts, sample_total, base):
    return pl.pallas_call(
        functools.partial(table_kernel, float(sample_total)),
        in_specs=[
            pl.BlockSpec(memory_space=pltpu.SMEM),
            pl.BlockSpec(memory_space=pltpu.VMEM),
        ],
        out_specs=pl.BlockSpec(memory_space=pltpu.VMEM),
        out_shape=jax.ShapeDtypeStruct(parts.shape, F32),
        compiler_params=vmem_params(16),
        name="rank_table",
    )(base, parts)


def lookup(bins, tables):
    lower = bins & 127
    values = [
        jnp.take_along_axis(table, lower, axis=1, mode="promise_in_bounds") for table in tables
    ]
    for bit in (128, 256, 512):
        odd = (bins & bit) != 0
        values = [jnp.where(odd, values[i + 1], values[i]) for i in range(0, len(values), 2)]
    return values[0]


def cross_kernel(
    bins_hbm, table_ref, dose_hbm, cov_hbm, plate_hbm, dproj_ref, dsq_ref,
    out_ref, bins_ref, cov_ref, plate_ref, dose_ref, level_ref, total_ref, design_ref, square_ref, sems,
):
    proteins, width = bins_hbm.shape
    chunk = dose_ref.shape[2]
    steps = width // chunk
    spans = [pl.ds(c * chunk, chunk) for c in range(steps)]
    bins_in = [
        pltpu.make_async_copy(
            bins_hbm.at[:, spans[c]], bins_ref.at[c], sems.at[c]
        )
        for c in range(steps)
    ]
    dose_in = [
        pltpu.make_async_copy(dose_hbm.at[:, spans[c]], dose_ref.at[c], sems.at[steps + c])
        for c in range(steps)
    ]
    rest_in = [
        pltpu.make_async_copy(cov_hbm, cov_ref, sems.at[2 * steps]),
        pltpu.make_async_copy(plate_hbm, plate_ref, sems.at[2 * steps + 1]),
    ]
    for copy in [bins_in[0], bins_in[1]] + rest_in + [dose_in[0]] + bins_in[2:] + dose_in[1:]:
        copy.start()
    square_ref[...] = jnp.zeros_like(square_ref)
    for c in range(steps):
        level_ref[c, 96:128, :] = jnp.zeros((32, chunk), BF16)
        level_ref[c, 224:256, :] = jnp.zeros((32, chunk), BF16)

    def levels(c):
        for g in range(0, 12, 2):
            pair = []
            for first in (g, g + 1):
                size = min(8, proteins - 8 * first)
                tables = [table_ref[pl.ds(64 * first + k, size, stride=8), :] for k in range(8)]
                pieces, squares = [], None
                for start in range(0, chunk, LANES):
                    bins = bins_ref[c, 8 * first : 8 * first + size, start : start + LANES]
                    value = lookup(bins, tables)
                    pieces.append(value)
                    squares = value * value if squares is None else squares + value * value
                square_ref[8 * first : 8 * first + size, :] += squares
                pieces = jnp.concatenate(pieces, axis=1)
                if size < 8:
                    pieces = jnp.concatenate([pieces, jnp.zeros((8 - size, chunk), F32)], axis=0)
                pair.append(pieces)
            value = jnp.concatenate(pair, axis=0)
            high = value.astype(BF16)
            low = (value - high.astype(F32)).astype(BF16)
            level_ref[c, 8 * g : 8 * g + 16, :] = high
            level_ref[c, 128 + 8 * g : 128 + 8 * g + 16, :] = low

    bins_in[0].wait()
    levels(0)
    for c in range(steps):
        dose_in[c].wait()
        if c == 0:
            for copy in rest_in:
                copy.wait()
        if c + 1 < steps:
            bins_in[c + 1].wait()
            levels(c + 1)
        level = level_ref[c]
        span = slice(c * chunk, (c + 1) * chunk)
        stack = jnp.concatenate(design_parts(cov_ref[:, span], plate_ref[:, span]), axis=0)
        design = lax.dot_general(stack, level, NT, preferred_element_type=F32)
        total = lax.dot_general(dose_ref[c], level, NT, preferred_element_type=F32)
        if c == 0:
            design_ref[...] = design
            total_ref[...] = total
        else:
            design_ref[...] += design
            total_ref[...] += total
    wide = design_ref[0:64, :] + design_ref[64:128, :] + design_ref[128:192, :]
    proj = wide[:, :LANES] + wide[:, LANES:]
    squares = lax.dot_general(
        jnp.ones((8, LANES), F32), square_ref[...], NT,
        precision=exact_mode, preferred_element_type=F32,
    )
    for x in range(4):
        rows = slice(256 * x, 256 * x + 256)
        out_ref[x, 0:256, :] = total_ref[rows, :LANES] + total_ref[rows, LANES:]
        out_ref[x, 256:384, :] = dproj_ref[128 * x : 128 * x + 128, :]
        out_ref[x, 384:448, :] = proj
        out_ref[x, 448:456, :] = squares
        out_ref[x, 450:452, :] = dsq_ref[2 * x : 2 * x + 2, :]


def cross_products(bin_ids, table, dosages, covariates, plates, dose_proj, dose_sq):
    count, width = dosages.shape
    chunk = CROSS_CHUNK
    steps = width // chunk
    whole = pl.BlockSpec(memory_space=pltpu.VMEM)
    hbm = pl.BlockSpec(memory_space=pl.ANY)
    return pl.pallas_call(
        cross_kernel,
        in_specs=[hbm, whole, hbm, hbm, hbm, whole, whole],
        out_specs=whole,
        out_shape=jax.ShapeDtypeStruct((4, 456, LANES), F32),
        scratch_shapes=[
            pltpu.VMEM((steps, bin_ids.shape[0], chunk), jnp.int32),
            pltpu.VMEM((COVARS, width), F32),
            pltpu.VMEM((1, width), jnp.int32),
            pltpu.VMEM((steps, count, chunk), BF16),
            pltpu.VMEM((steps, 256, chunk), BF16),
            pltpu.VMEM((count, 256), F32),
            pltpu.VMEM((192, 256), F32),
            pltpu.VMEM((LANES, LANES), F32),
            pltpu.SemaphoreType.DMA((2 * steps + 2,)),
        ],
        compiler_params=vmem_params(60),
        name="cross_products",
    )(bin_ids, table, dosages, covariates, plates, dose_proj, dose_sq)


def regroup_kernel(parts_ref, out_ref):
    total = parts_ref[0] + parts_ref[1] + parts_ref[2] + parts_ref[3]
    row = lax.broadcasted_iota(jnp.int32, (8, LANES), 0)
    for z in range(8):
        out_ref[z, 0:32, :] = total[32 * z : 32 * z + 32]
        out_ref[z, 32:48, :] = total[256 + 16 * z : 256 + 16 * z + 16]
        out_ref[z, 48:112, :] = total[384:448]
        squares = total[448:456]
        own = squares[2 + z // 4 : 3 + z // 4]
        own = pltpu.roll(own, (4 - z % 4) % 4 * 32, 1) if z % 4 else own
        out_ref[z, 112:120, :] = jnp.where(row == 1, own, squares)


def regroup(parts):
    whole = pl.BlockSpec(memory_space=pltpu.VMEM)
    return pl.pallas_call(
        regroup_kernel,
        in_specs=[whole],
        out_specs=whole,
        out_shape=jax.ShapeDtypeStruct((8, 120, LANES), F32),
        compiler_params=vmem_params(16),
        name="regroup",
    )(parts)


def finish_kernel(freedom, parts_ref, inverse_ref, out_ref):
    total = parts_ref[0]
    for z in range(1, 8):
        total = total + parts_ref[z]
    cross, dose, proj, squares = total[0:32], total[32:48], total[48:112], total[112:113]
    shape = (32, LANES)
    diagonal = lax.broadcasted_iota(jnp.int32, shape, 0) == lane_ids(shape)
    dose_squares = jnp.sum(
        jnp.where(diagonal, jnp.broadcast_to(total[113:114], shape), 0.0), axis=1, keepdims=True
    )
    inverse = inverse_ref[...]
    dot = functools.partial(
        lax.dot_general, precision=exact_mode, preferred_element_type=F32
    )
    expr_white = dot(inverse, proj, NN)
    dose_both = jnp.concatenate([dose[:, :64], dose[:, 64:]], axis=0)
    dose_white = dot(dose_both, inverse, NT)
    expr_norm = squares - jnp.sum(expr_white * expr_white, axis=0, keepdims=True)
    dose_norm = dose_squares - jnp.sum(dose_white * dose_white, axis=1, keepdims=True)
    cross = cross - dot(dose_white, expr_white, NN)
    corr = cross * lax.rsqrt(dose_norm * expr_norm + tiny_eps)
    stats = corr * jnp.sqrt(freedom / (1.0 - corr * corr))
    out_ref[...] = stats[:, : out_ref.shape[1]]


def finish(parts, inverse, freedom, proteins):
    whole = pl.BlockSpec(memory_space=pltpu.VMEM)
    return pl.pallas_call(
        functools.partial(finish_kernel, float(freedom)),
        in_specs=[whole, whole],
        out_specs=whole,
        out_shape=jax.ShapeDtypeStruct((32, proteins), F32),
        compiler_params=vmem_params(16),
        name="finish",
    )(parts, inverse)


def body(bin_ids, plate_ids, covariates, dosages):
    sample_total = bin_ids.shape[1] * lax.axis_size("samp")
    plates = plate_ids[None, :]
    x_groups = [[x * 8 + z for x in range(4)] for z in range(8)]
    z_groups = [[x * 8 + z for z in range(8)] for x in range(4)]
    base = (lax.axis_index("samp") * 24).astype(jnp.int32)[None]

    counts = histogram(bin_ids, covariates, plates).reshape(32, 24, LANES)
    counts = lax.all_to_all(counts, "samp", 0, 0, tiled=True)
    dose_proj, dose_sq = dose_products(dosages, covariates, plates)
    counts, dose_proj, dose_sq = lax.optimization_barrier((counts, dose_proj, dose_sq))
    table = rank_table(counts, sample_total, base)
    table = lax.all_to_all(table, "samp", 0, 0, tiled=True).reshape(768, LANES)
    parts = cross_products(bin_ids, table, dosages, covariates, plates, dose_proj, dose_sq)
    packed, parts = lax.optimization_barrier((table[736:], parts))
    gram = jnp.concatenate([packed[:, :64], packed[:, 64:]], axis=0)
    factor = lax.linalg.cholesky(gram, symmetrize_input=False)
    parts = lax.all_to_all(parts, "samp", 0, 0, axis_index_groups=x_groups, tiled=True)
    parts, factor = lax.optimization_barrier((parts, factor))
    inverse = lax.linalg.triangular_solve(
        factor, jnp.eye(DESIGN, dtype=F32), left_side=True, lower=True
    )
    parts = regroup(parts)
    parts = lax.all_to_all(parts, "samp", 0, 0, axis_index_groups=z_groups, tiled=True)
    return finish(parts, inverse, sample_total - DESIGN - 1.0, bin_ids.shape[0])


def solution(mesh):
    placed = (P("prot", "samp"), P("samp"), P(None, "samp"), P(None, "samp"))
    return jax.shard_map(
        body, mesh=mesh, in_specs=placed, out_specs=P("samp", "prot"), check_vma=False
    )
```

```python
import functools
import math

import jax
import jax.numpy as jnp
from jax import lax
from jax.experimental import pallas as pl
from jax.experimental.pallas import tpu as pltpu
from jax.sharding import PartitionSpec as P

BINS = 1024
PLATES = 24
COVARS = 40
DESIGN = 64
DOSE_CHUNK = 1024
CROSS_CHUNK = 1024
LANES = 128
tiny_eps = 1e-06
F32 = jnp.float32
BF16 = jnp.bfloat16
FP8 = jnp.float8_e4m3fn
exact_mode = lax.Precision.HIGHEST
NT = (((1,), (1,)), ((), ()))
NN = (((1,), (0,)), ((), ()))


def vmem_params(mib):
    return pltpu.CompilerParams(vmem_limit_bytes=mib * 1024 * 1024)


def lane_ids(shape):
    return lax.broadcasted_iota(jnp.int32, shape, len(shape) - 1)


def design_parts(cov, plates):
    width = cov.shape[1]
    rows = lax.broadcasted_iota(jnp.int32, (PLATES, width), 0)
    plate_rows = jnp.where(plates == rows, 1.0, 0.0).astype(F32)
    design = jnp.concatenate([cov, plate_rows], axis=0)
    high = design.astype(BF16)
    rest = design - high.astype(F32)
    middle = rest.astype(BF16)
    low = (rest - middle.astype(F32)).astype(BF16)
    return high, middle, low


def fold_lanes(wide):
    first, second = wide[:, :LANES], wide[:, LANES:]
    pair = first + second
    return pair + pltpu.roll(pair, 64, 1)


WAITS = {0: (0, 1), 2: tuple(range(2, 14))}


def hist_kernel(bins_hbm, cov_hbm, plate_hbm, out_ref, bins_ref, cov_ref, plate_ref, table_ref, sems):
    proteins, width = bins_hbm.shape
    chunk = 1024
    groups = [(start, min(8, proteins - start)) for start in range(0, proteins, 8)]
    copies = [
        pltpu.make_async_copy(
            bins_hbm.at[pl.ds(start, size)], bins_ref.at[pl.ds(start, size)], sems.at[n]
        )
        for n, (start, size) in enumerate(groups)
    ]
    copies.append(pltpu.make_async_copy(cov_hbm, cov_ref, sems.at[len(groups)]))
    copies.append(pltpu.make_async_copy(plate_hbm, plate_ref, sems.at[len(groups) + 1]))
    for copy in copies:
        copy.start()
    ids = lax.broadcasted_iota(jnp.int32, (32, chunk), 0).astype(jnp.int8)
    one = jnp.ones((32, chunk), F32).astype(FP8)
    zero = jnp.zeros((32, chunk), F32).astype(FP8)
    block = lane_ids((8, LANES)) // 32
    for n, (first, size) in enumerate(groups):
        for k in WAITS.get(n, ()):
            copies[k].wait()
        side = 32 * size
        total = jnp.zeros((side, side), F32)
        for start in range(0, width, chunk):
            bins = bins_ref[first : first + size, start : start + chunk]
            left, right = [], []
            for p in range(size):
                row = jnp.broadcast_to(bins[p : p + 1], (32, chunk))
                left.append(jnp.where((row >> 5).astype(jnp.int8) == ids, one, zero))
                right.append(jnp.where((row & 31).astype(jnp.int8) == ids, one, zero))
            total = total + lax.dot_general(
                jnp.concatenate(left, axis=0),
                jnp.concatenate(right, axis=0),
                NT,
                preferred_element_type=F32,
            )
        lane = lane_ids((32, side)) // 32
        diag = total[:32]
        for p in range(1, size):
            diag = jnp.where(lane == p, total[32 * p : 32 * p + 32], diag)
        for half in range(side // LANES):
            table_ref[n % 2, half] = diag[:, half * LANES : (half + 1) * LANES]
            rows = [table_ref[n % 2, half, pl.ds(c, 8, stride=4), :] for c in range(4)]
            for q in range(4):
                out = rows[q]
                for c in range(4):
                    shift = ((c - q) % 4) * 32
                    moved = pltpu.roll(rows[c], shift, 1) if shift else rows[c]
                    out = jnp.where(block == c, moved, out)
                p = first + half * 4 + q
                out_ref[8 * p : 8 * p + 8, :] = out
    high, middle, low = design_parts(cov_ref[...], plate_ref[...])
    stack = jnp.concatenate([high, middle, low, jnp.zeros_like(high)], axis=0)
    wide = lax.dot_general(stack[:192], stack, NT, preferred_element_type=F32)
    gram = fold_lanes(wide[:64] + wide[64:128] + wide[128:192])
    out_ref[8 * proteins :, :] = jnp.where(lane_ids((32, LANES)) < 64, gram[:32], gram[32:])


def histogram(bin_ids, covariates, plates):
    proteins, width = bin_ids.shape
    hbm = pl.BlockSpec(memory_space=pl.ANY)
    return pl.pallas_call(
        hist_kernel,
        in_specs=[hbm, hbm, hbm],
        out_specs=pl.BlockSpec(memory_space=pltpu.VMEM),
        out_shape=jax.ShapeDtypeStruct((768, LANES), F32),
        scratch_shapes=[
            pltpu.VMEM((96, width), jnp.int32),
            pltpu.VMEM((COVARS, width), F32),
            pltpu.VMEM((1, width), jnp.int32),
            pltpu.VMEM((2, 2, 32, LANES), F32),
            pltpu.SemaphoreType.DMA((14,)),
        ],
        compiler_params=vmem_params(60),
        name="histogram",
    )(bin_ids, covariates, plates)


def dose_kernel(dose_hbm, cov_ref, plate_ref, proj_ref, dose_ref, total_ref, part_ref, sems):
    chunk = dose_ref.shape[2]
    copies = [
        pltpu.make_async_copy(
            dose_hbm.at[:, pl.ds(c * chunk, chunk)], dose_ref.at[c], sems.at[c]
        )
        for c in range(dose_ref.shape[0])
    ]
    for copy in copies:
        copy.start()
    high, middle, low = design_parts(cov_ref[...], plate_ref[...])
    stack = jnp.concatenate([high, middle, low, jnp.zeros_like(high)], axis=0)
    for c in range(len(copies)):
        copies[c].wait()
        for r in range(0, dose_ref.shape[1], 256):
            dose = dose_ref[c, r : r + 256, :]
            term = lax.dot_general(
                dose, stack[:, c * chunk : (c + 1) * chunk], NT, preferred_element_type=F32
            )
            wide = dose.astype(F32)
            wide = wide * wide
            part = wide[:, :LANES]
            for start in range(LANES, chunk, LANES):
                part = part + wide[:, start : start + LANES]
            if c == 0:
                total_ref[r : r + 256, :] = term
                part_ref[r : r + 256, :] = part
            else:
                total_ref[r : r + 256, :] += term
                part_ref[r : r + 256, :] += part
    for c in range(proj_ref.shape[1] // LANES):
        span = slice(LANES * c, LANES * (c + 1))
        proj_ref[0:64, span] = fold_lanes(total_ref[span, :]).T[:64]
    squares = lax.dot_general(
        jnp.ones((8, LANES), F32), part_ref[...], NT,
        precision=exact_mode, preferred_element_type=F32,
    )
    proj_ref[64:72, :] = squares


def dose_products(dosages, covariates, plates):
    count, width = dosages.shape
    chunk = DOSE_CHUNK
    whole = pl.BlockSpec(memory_space=pltpu.VMEM)
    return pl.pallas_call(
        dose_kernel,
        in_specs=[pl.BlockSpec(memory_space=pl.ANY), whole, whole],
        out_specs=whole,
        out_shape=jax.ShapeDtypeStruct((DESIGN + 8, count), F32),
        scratch_shapes=[
            pltpu.VMEM((width // chunk, count, chunk), BF16),
            pltpu.VMEM((count, 256), F32),
            pltpu.VMEM((count, LANES), F32),
            pltpu.SemaphoreType.DMA((width // chunk,)),
        ],
        compiler_params=vmem_params(50),
        cost_estimate=pl.CostEstimate(
            flops=2 * count * width * 256, bytes_accessed=count * width * 2, transcendentals=0
        ),
        name="dose_products",
    )(dosages, covariates, plates)


def erf_inverse(x):
    w = -jnp.log1p(-x * x)
    small = w < 5.0
    shifted = jnp.where(small, w - 2.5, jnp.sqrt(w) - 3.0)
    near = (
        2.81022636e-08, 3.43273939e-07, -3.5233877e-06, -4.39150654e-06, 0.00021858087,
        -0.00125372503, -0.00417768164, 0.246640727, 1.50140941,
    )
    far = (
        -0.000200214257, 0.000100950558, 0.00134934322, -0.00367342844, 0.00573950773,
        -0.0076224613, 0.00943887047, 1.00167406, 2.83297682,
    )
    value = jnp.where(small, near[0], far[0])
    for a, b in zip(near[1:], far[1:]):
        value = value * shifted + jnp.where(small, a, b)
    return value * x


def table_kernel(sample_total, base_ref, parts_ref, out_ref):
    counts = jnp.sum(parts_ref[...], axis=0)
    rows = counts.shape[0]
    row = lax.broadcasted_iota(jnp.int32, (LANES, LANES), 0)
    before = (row < lane_ids((LANES, LANES))).astype(F32)
    inside = lax.dot_general(
        counts, before, NN, precision=exact_mode, preferred_element_type=F32
    )
    totals = jnp.broadcast_to(jnp.sum(counts, axis=1, keepdims=True), counts.shape)
    row = lax.broadcasted_iota(jnp.int32, (rows, rows), 0)
    col = lane_ids((rows, rows))
    earlier = ((col < row) & (col // 8 == row // 8)).astype(F32)
    outside = lax.dot_general(
        earlier, totals, NN, precision=exact_mode, preferred_element_type=F32
    )
    middle = inside + outside + 0.5 * (counts + 1.0)
    level = (middle - 0.375) / (sample_total + 0.25)
    values = math.sqrt(2.0) * erf_inverse(2.0 * level - 1.0)
    place = base_ref[0] + lax.broadcasted_iota(jnp.int32, counts.shape, 0)
    values = jnp.where(place < 736, values, counts)
    for n in range(out_ref.shape[0]):
        out_ref[n] = values


def rank_table(parts, sample_total, base):
    return pl.pallas_call(
        functools.partial(table_kernel, float(sample_total)),
        in_specs=[
            pl.BlockSpec(memory_space=pltpu.SMEM),
            pl.BlockSpec(memory_space=pltpu.VMEM),
        ],
        out_specs=pl.BlockSpec(memory_space=pltpu.VMEM),
        out_shape=jax.ShapeDtypeStruct(parts.shape, F32),
        compiler_params=vmem_params(8),
        name="rank_table",
    )(base, parts)


def lookup(bins, tables):
    lower = bins & 127
    values = [
        jnp.take_along_axis(table, lower, axis=1, mode="promise_in_bounds") for table in tables
    ]
    for bit in (128, 256, 512):
        odd = (bins & bit) != 0
        values = [jnp.where(odd, values[i + 1], values[i]) for i in range(0, len(values), 2)]
    return values[0]


def cross_kernel(
    bins_hbm, table_ref, dose_hbm, cov_hbm, plate_hbm, dproj_ref,
    out_ref, bins_ref, cov_ref, plate_ref, dose_ref, level_ref, total_ref, design_ref, square_ref, sems,
):
    proteins, width = bins_hbm.shape
    chunk = dose_ref.shape[2]
    steps = width // chunk
    spans = [pl.ds(c * chunk, chunk) for c in range(steps)]
    bins_in = [
        pltpu.make_async_copy(
            bins_hbm.at[:, spans[c]], bins_ref.at[c], sems.at[c]
        )
        for c in range(steps)
    ]
    dose_in = [
        pltpu.make_async_copy(dose_hbm.at[:, spans[c]], dose_ref.at[c], sems.at[steps + c])
        for c in range(steps)
    ]
    rest_in = [
        pltpu.make_async_copy(cov_hbm, cov_ref, sems.at[2 * steps]),
        pltpu.make_async_copy(plate_hbm, plate_ref, sems.at[2 * steps + 1]),
    ]
    for copy in [bins_in[0], bins_in[1]] + rest_in + [dose_in[0]] + bins_in[2:] + dose_in[1:]:
        copy.start()
    square_ref[...] = jnp.zeros_like(square_ref)
    for c in range(steps):
        level_ref[c, 96:128, :] = jnp.zeros((32, chunk), BF16)
        level_ref[c, 224:256, :] = jnp.zeros((32, chunk), BF16)

    def levels(c):
        for g in range(0, 12, 2):
            pair = []
            for first in (g, g + 1):
                size = min(8, proteins - 8 * first)
                tables = [table_ref[pl.ds(64 * first + k, size, stride=8), :] for k in range(8)]
                pieces, squares = [], None
                for start in range(0, chunk, LANES):
                    bins = bins_ref[c, 8 * first : 8 * first + size, start : start + LANES]
                    value = lookup(bins, tables)
                    pieces.append(value)
                    squares = value * value if squares is None else squares + value * value
                square_ref[8 * first : 8 * first + size, :] += squares
                pieces = jnp.concatenate(pieces, axis=1)
                if size < 8:
                    pieces = jnp.concatenate([pieces, jnp.zeros((8 - size, chunk), F32)], axis=0)
                pair.append(pieces)
            value = jnp.concatenate(pair, axis=0)
            high = value.astype(BF16)
            low = (value - high.astype(F32)).astype(BF16)
            level_ref[c, 8 * g : 8 * g + 16, :] = high
            level_ref[c, 128 + 8 * g : 128 + 8 * g + 16, :] = low

    bins_in[0].wait()
    levels(0)
    for c in range(steps):
        dose_in[c].wait()
        if c == 0:
            for copy in rest_in:
                copy.wait()
        if c + 1 < steps:
            bins_in[c + 1].wait()
            levels(c + 1)
        level = level_ref[c]
        span = slice(c * chunk, (c + 1) * chunk)
        stack = jnp.concatenate(design_parts(cov_ref[:, span], plate_ref[:, span]), axis=0)
        design = lax.dot_general(stack, level, NT, preferred_element_type=F32)
        total = lax.dot_general(dose_ref[c], level, NT, preferred_element_type=F32)
        if c == 0:
            design_ref[...] = design
            total_ref[...] = total
        else:
            design_ref[...] += design
            total_ref[...] += total
    wide = design_ref[0:64, :] + design_ref[64:128, :] + design_ref[128:192, :]
    proj = wide[:, :LANES] + wide[:, LANES:]
    squares = lax.dot_general(
        jnp.ones((8, LANES), F32), square_ref[...], NT,
        precision=exact_mode, preferred_element_type=F32,
    )
    spare = lane_ids((64, LANES)) >= 96
    own = [pltpu.roll(squares[0:1], shift, 1) for shift in (96, 64, 32)]
    for x in range(4):
        rows = slice(256 * x, 256 * x + 256)
        out_ref[x, 0:256, :] = total_ref[rows, :LANES] + total_ref[rows, LANES:]
        out_ref[x, 256:320, :] = dproj_ref[0:64, 256 * x : 256 * x + 128]
        out_ref[x, 320:384, :] = dproj_ref[0:64, 256 * x + 128 : 256 * x + 256]
        dose_own = []
        for z in range(8):
            first = 256 * x + LANES * (z // 4)
            row = dproj_ref[64:65, first : first + LANES]
            dose_own.append(pltpu.roll(row, 96 - 32 * (z % 4), 1) if z % 4 < 3 else row)
        pieces = jnp.concatenate(own + dose_own + [jnp.zeros((53, LANES), F32)], axis=0)
        out_ref[x, 384:448, :] = jnp.where(spare, pieces, proj)


def cross_products(bin_ids, table, dosages, covariates, plates, dose_proj):
    count, width = dosages.shape
    chunk = CROSS_CHUNK
    steps = width // chunk
    whole = pl.BlockSpec(memory_space=pltpu.VMEM)
    hbm = pl.BlockSpec(memory_space=pl.ANY)
    return pl.pallas_call(
        cross_kernel,
        in_specs=[hbm, whole, hbm, hbm, hbm, whole],
        out_specs=whole,
        out_shape=jax.ShapeDtypeStruct((4, 448, LANES), F32),
        scratch_shapes=[
            pltpu.VMEM((steps, bin_ids.shape[0], chunk), jnp.int32),
            pltpu.VMEM((COVARS, width), F32),
            pltpu.VMEM((1, width), jnp.int32),
            pltpu.VMEM((steps, count, chunk), BF16),
            pltpu.VMEM((steps, 256, chunk), BF16),
            pltpu.VMEM((count, 256), F32),
            pltpu.VMEM((192, 256), F32),
            pltpu.VMEM((LANES, LANES), F32),
            pltpu.SemaphoreType.DMA((2 * steps + 2,)),
        ],
        compiler_params=vmem_params(50),
        name="cross_products",
    )(bin_ids, table, dosages, covariates, plates, dose_proj)


def regroup_kernel(parts_ref, out_ref):
    total = parts_ref[0] + parts_ref[1] + parts_ref[2] + parts_ref[3]
    proj = total[384:448]
    for z in range(8):
        squares = jnp.concatenate(
            [proj[0:3], proj[3 + z : 4 + z], jnp.zeros((28, LANES), F32)], axis=0
        )
        cross = total[32 * z : 32 * z + 32]
        out_ref[z, 0:32, :] = jnp.where(lane_ids((32, LANES)) >= 96, squares, cross)
        dose = total[256 + 64 * (z // 4) : 320 + 64 * (z // 4)]
        dose = pltpu.roll(dose, 96 - 32 * (z % 4), 1) if z % 4 < 3 else dose
        out_ref[z, 32:96, :] = jnp.where(lane_ids((64, LANES)) >= 96, dose, proj)


def regroup(parts):
    whole = pl.BlockSpec(memory_space=pltpu.VMEM)
    return pl.pallas_call(
        regroup_kernel,
        in_specs=[whole],
        out_specs=whole,
        out_shape=jax.ShapeDtypeStruct((8, 96, LANES), F32),
        compiler_params=vmem_params(8),
        name="regroup",
    )(parts)


def inverse_kernel(gram_ref, out_ref):
    packed = gram_ref[...]
    lane = lane_ids((DESIGN, LANES))
    row = lax.broadcasted_iota(jnp.int32, (DESIGN, LANES), 0)
    work = jnp.concatenate([packed, pltpu.roll(packed, 64, 1)], axis=0)
    work = jnp.where(lane < DESIGN, work, jnp.where(lane == row + DESIGN, 1.0, 0.0))
    plate = work[COVARS:]
    low_lane = lane_ids((PLATES, LANES))
    low_row = lax.broadcasted_iota(jnp.int32, (PLATES, LANES), 0)
    pivots = jnp.sum(
        jnp.where(low_lane == low_row + COVARS, plate, 0.0), axis=1, keepdims=True
    )
    upper = work[:COVARS]
    coupling = upper[:, COVARS:DESIGN]
    upper = upper - lax.dot_general(
        coupling, plate * (1.0 / pivots), NN, precision=exact_mode, preferred_element_type=F32
    )
    for k in range(COVARS):
        first = k // 8 * 8
        source = upper[k : k + 1]
        rest = upper[first:]
        scale = 1.0 / source[:, k : k + 1]
        below = lax.broadcasted_iota(jnp.int32, rest.shape, 0) > k - first
        factor = jnp.where(below, rest[:, k : k + 1] * (source * scale), 0.0)
        rest = rest - factor
        upper = jnp.concatenate([upper[:first], rest], axis=0) if first else rest
    work = jnp.concatenate([upper, plate], axis=0)
    diagonal = jnp.sum(jnp.where(lane == row, work, 0.0), axis=1, keepdims=True)
    out_ref[...] = pltpu.roll(work * lax.rsqrt(diagonal), 64, 1)[:, :DESIGN]


def inverse_factor(table):
    return pl.pallas_call(
        inverse_kernel,
        grid=(1,),
        in_specs=[pl.BlockSpec((32, LANES), lambda i: (23, 0))],
        out_specs=pl.BlockSpec((DESIGN, DESIGN), lambda i: (0, 0)),
        out_shape=jax.ShapeDtypeStruct((DESIGN, DESIGN), F32),
        compiler_params=vmem_params(8),
        cost_estimate=pl.CostEstimate(flops=4_000_000_000, bytes_accessed=32768, transcendentals=0),
        name="inverse_factor",
    )(table)


def finish_kernel(freedom, parts_ref, inverse_ref, out_ref):
    total = parts_ref[0]
    for z in range(1, 8):
        total = total + parts_ref[z]
    shape = (32, LANES)
    lane = lane_ids((1, LANES))
    white = lax.dot_general(
        inverse_ref[...], total[32:96], NN, precision=exact_mode, preferred_element_type=F32
    )
    shared = lax.dot_general(
        white, white, (((0,), (0,)), ((), ())), precision=exact_mode, preferred_element_type=F32
    )
    removed = jnp.sum(white * white, axis=0, keepdims=True)
    expr_sq = [pltpu.roll(total[j : j + 1], 32 * j + 32, 1) for j in range(3)]
    expr_sq = jnp.where(lane < 32, expr_sq[0], jnp.where(lane < 64, expr_sq[1], expr_sq[2]))
    expr_norm = expr_sq - removed
    own = lane_ids(shape) == lax.broadcasted_iota(jnp.int32, shape, 0) + 96
    dose_norm = jnp.broadcast_to(total[3:4] - removed, shape)
    dose_norm = jnp.sum(jnp.where(own, dose_norm, 0.0), axis=1, keepdims=True)
    cross = total[0:32] - shared[96:128]
    corr = cross * lax.rsqrt(dose_norm * expr_norm + tiny_eps)
    stats = corr * jnp.sqrt(freedom / (1.0 - corr * corr))
    out_ref[...] = stats[:, : out_ref.shape[1]]


def finish(parts, inverse, freedom, proteins):
    whole = pl.BlockSpec(memory_space=pltpu.VMEM)
    return pl.pallas_call(
        functools.partial(finish_kernel, float(freedom)),
        in_specs=[whole, whole],
        out_specs=whole,
        out_shape=jax.ShapeDtypeStruct((32, proteins), F32),
        compiler_params=vmem_params(8),
        name="finish",
    )(parts, inverse)


def body(bin_ids, plate_ids, covariates, dosages):
    sample_total = bin_ids.shape[1] * lax.axis_size("samp")
    plates = plate_ids[None, :]
    x_groups = [[x * 8 + z for x in range(4)] for z in range(8)]
    z_groups = [[x * 8 + z for z in range(8)] for x in range(4)]
    base = (lax.axis_index("samp") * 24).astype(jnp.int32)[None]

    counts = histogram(bin_ids, covariates, plates).reshape(32, 24, LANES)
    counts = lax.all_to_all(counts, "samp", 0, 0, tiled=True)
    dose_proj = dose_products(dosages, covariates, plates)
    counts, dose_proj = lax.optimization_barrier((counts, dose_proj))
    table = rank_table(counts, sample_total, base)
    table = lax.all_to_all(table, "samp", 0, 0, tiled=True).reshape(768, LANES)
    parts = cross_products(bin_ids, table, dosages, covariates, plates, dose_proj)
    late_table, parts = lax.optimization_barrier((table, parts))
    inverse = inverse_factor(late_table)
    parts = lax.all_to_all(parts, "samp", 0, 0, axis_index_groups=x_groups, tiled=True)
    parts, inverse = lax.optimization_barrier((parts, inverse))
    parts = regroup(parts)
    parts = lax.all_to_all(parts, "samp", 0, 0, axis_index_groups=z_groups, tiled=True)
    return finish(parts, inverse, sample_total - DESIGN - 1.0, bin_ids.shape[0])


def solution(mesh):
    placed = (P("prot", "samp"), P("samp"), P(None, "samp"), P(None, "samp"))
    return jax.shard_map(
        body, mesh=mesh, in_specs=placed, out_specs=P("samp", "prot"), check_vma=False
    )
```

```python
import functools
import math

import jax
import jax.numpy as jnp
from jax import lax
from jax.experimental import pallas as pl
from jax.experimental.pallas import tpu as pltpu
from jax.sharding import PartitionSpec as P

BINS = 1024
PLATES = 24
COVARS = 40
DESIGN = 64
DOSE_CHUNK = 1024
CROSS_CHUNK = 1024
LANES = 128
tiny_eps = 1e-06
F32 = jnp.float32
BF16 = jnp.bfloat16
FP8 = jnp.float8_e4m3fn
exact_mode = lax.Precision.HIGHEST
NT = (((1,), (1,)), ((), ()))
NN = (((1,), (0,)), ((), ()))


def vmem_params(mib):
    return pltpu.CompilerParams(vmem_limit_bytes=mib * 1024 * 1024)


def lane_ids(shape):
    return lax.broadcasted_iota(jnp.int32, shape, len(shape) - 1)


def design_parts(cov, plates):
    width = cov.shape[1]
    rows = lax.broadcasted_iota(jnp.int32, (PLATES, width), 0)
    plate_rows = jnp.where(plates == rows, 1.0, 0.0).astype(F32)
    design = jnp.concatenate([cov, plate_rows], axis=0)
    high = design.astype(BF16)
    rest = design - high.astype(F32)
    middle = rest.astype(BF16)
    low = (rest - middle.astype(F32)).astype(BF16)
    return high, middle, low


def fold_lanes(wide):
    first, second = wide[:, :LANES], wide[:, LANES:]
    pair = first + second
    return pair + pltpu.roll(pair, 64, 1)


WAITS = {0: (0, 1), 2: tuple(range(2, 14))}


def hist_kernel(bins_hbm, cov_hbm, plate_hbm, out_ref, bins_ref, cov_ref, plate_ref, table_ref, sems):
    proteins, width = bins_hbm.shape
    chunk = 1024
    groups = [(start, min(8, proteins - start)) for start in range(0, proteins, 8)]
    copies = [
        pltpu.make_async_copy(
            bins_hbm.at[pl.ds(start, size)], bins_ref.at[pl.ds(start, size)], sems.at[n]
        )
        for n, (start, size) in enumerate(groups)
    ]
    copies.append(pltpu.make_async_copy(cov_hbm, cov_ref, sems.at[len(groups)]))
    copies.append(pltpu.make_async_copy(plate_hbm, plate_ref, sems.at[len(groups) + 1]))
    for copy in copies:
        copy.start()
    ids = lax.broadcasted_iota(jnp.int32, (32, chunk), 0).astype(jnp.int8)
    one = jnp.ones((32, chunk), F32).astype(FP8)
    zero = jnp.zeros((32, chunk), F32).astype(FP8)
    block = lane_ids((8, LANES)) // 32
    for n, (first, size) in enumerate(groups):
        for k in WAITS.get(n, ()):
            copies[k].wait()
        side = 32 * size
        total = jnp.zeros((side, side), F32)
        for start in range(0, width, chunk):
            bins = bins_ref[first : first + size, start : start + chunk]
            left, right = [], []
            for p in range(size):
                row = jnp.broadcast_to(bins[p : p + 1], (32, chunk))
                left.append(jnp.where((row >> 5).astype(jnp.int8) == ids, one, zero))
                right.append(jnp.where((row & 31).astype(jnp.int8) == ids, one, zero))
            total = total + lax.dot_general(
                jnp.concatenate(left, axis=0),
                jnp.concatenate(right, axis=0),
                NT,
                preferred_element_type=F32,
            )
        lane = lane_ids((32, side)) // 32
        diag = total[:32]
        for p in range(1, size):
            diag = jnp.where(lane == p, total[32 * p : 32 * p + 32], diag)
        for half in range(side // LANES):
            table_ref[n % 2, half] = diag[:, half * LANES : (half + 1) * LANES]
            rows = [table_ref[n % 2, half, pl.ds(c, 8, stride=4), :] for c in range(4)]
            for q in range(4):
                out = rows[q]
                for c in range(4):
                    shift = ((c - q) % 4) * 32
                    moved = pltpu.roll(rows[c], shift, 1) if shift else rows[c]
                    out = jnp.where(block == c, moved, out)
                p = first + half * 4 + q
                out_ref[8 * p : 8 * p + 8, :] = out
    high, middle, low = design_parts(cov_ref[...], plate_ref[...])
    stack = jnp.concatenate([high, middle, low, jnp.zeros_like(high)], axis=0)
    wide = lax.dot_general(stack[:192], stack, NT, preferred_element_type=F32)
    gram = fold_lanes(wide[:64] + wide[64:128] + wide[128:192])
    out_ref[8 * proteins :, :] = jnp.where(lane_ids((32, LANES)) < 64, gram[:32], gram[32:])


def histogram(bin_ids, covariates, plates):
    proteins, width = bin_ids.shape
    hbm = pl.BlockSpec(memory_space=pl.ANY)
    return pl.pallas_call(
        hist_kernel,
        in_specs=[hbm, hbm, hbm],
        out_specs=pl.BlockSpec(memory_space=pltpu.VMEM),
        out_shape=jax.ShapeDtypeStruct((768, LANES), F32),
        scratch_shapes=[
            pltpu.VMEM((96, width), jnp.int32),
            pltpu.VMEM((COVARS, width), F32),
            pltpu.VMEM((1, width), jnp.int32),
            pltpu.VMEM((2, 2, 32, LANES), F32),
            pltpu.SemaphoreType.DMA((14,)),
        ],
        compiler_params=vmem_params(60),
        name="histogram",
    )(bin_ids, covariates, plates)


def dose_kernel(dose_hbm, cov_ref, plate_ref, proj_ref, dose_ref, total_ref, part_ref, sems):
    chunk = dose_ref.shape[2]
    copies = [
        pltpu.make_async_copy(
            dose_hbm.at[:, pl.ds(c * chunk, chunk)], dose_ref.at[c], sems.at[c]
        )
        for c in range(dose_ref.shape[0])
    ]
    for copy in copies:
        copy.start()
    high, middle, low = design_parts(cov_ref[...], plate_ref[...])
    stack = jnp.concatenate([high, middle, low, jnp.zeros_like(high)], axis=0)
    for c in range(len(copies)):
        copies[c].wait()
        for r in range(0, dose_ref.shape[1], 256):
            dose = dose_ref[c, r : r + 256, :]
            term = lax.dot_general(
                dose, stack[:, c * chunk : (c + 1) * chunk], NT, preferred_element_type=F32
            )
            wide = dose.astype(F32)
            wide = wide * wide
            part = wide[:, :LANES]
            for start in range(LANES, chunk, LANES):
                part = part + wide[:, start : start + LANES]
            if c == 0:
                total_ref[r : r + 256, :] = term
                part_ref[r : r + 256, :] = part
            else:
                total_ref[r : r + 256, :] += term
                part_ref[r : r + 256, :] += part
    for c in range(proj_ref.shape[1] // LANES):
        span = slice(LANES * c, LANES * (c + 1))
        proj_ref[0:64, span] = fold_lanes(total_ref[span, :]).T[:64]
    squares = lax.dot_general(
        jnp.ones((8, LANES), F32), part_ref[...], NT,
        precision=exact_mode, preferred_element_type=F32,
    )
    proj_ref[64:72, :] = squares


def dose_products(dosages, covariates, plates):
    count, width = dosages.shape
    chunk = DOSE_CHUNK
    whole = pl.BlockSpec(memory_space=pltpu.VMEM)
    return pl.pallas_call(
        dose_kernel,
        in_specs=[pl.BlockSpec(memory_space=pl.ANY), whole, whole],
        out_specs=whole,
        out_shape=jax.ShapeDtypeStruct((DESIGN + 8, count), F32),
        scratch_shapes=[
            pltpu.VMEM((width // chunk, count, chunk), BF16),
            pltpu.VMEM((count, 256), F32),
            pltpu.VMEM((count, LANES), F32),
            pltpu.SemaphoreType.DMA((width // chunk,)),
        ],
        compiler_params=vmem_params(50),
        cost_estimate=pl.CostEstimate(
            flops=2 * count * width * 256, bytes_accessed=count * width * 2, transcendentals=0
        ),
        name="dose_products",
    )(dosages, covariates, plates)


def erf_inverse(x):
    w = -jnp.log1p(-x * x)
    small = w < 5.0
    shifted = jnp.where(small, w - 2.5, jnp.sqrt(w) - 3.0)
    near = (
        2.81022636e-08, 3.43273939e-07, -3.5233877e-06, -4.39150654e-06, 0.00021858087,
        -0.00125372503, -0.00417768164, 0.246640727, 1.50140941,
    )
    far = (
        -0.000200214257, 0.000100950558, 0.00134934322, -0.00367342844, 0.00573950773,
        -0.0076224613, 0.00943887047, 1.00167406, 2.83297682,
    )
    value = jnp.where(small, near[0], far[0])
    for a, b in zip(near[1:], far[1:]):
        value = value * shifted + jnp.where(small, a, b)
    return value * x


def table_kernel(sample_total, base_ref, parts_ref, out_ref):
    counts = jnp.sum(parts_ref[...], axis=0)
    rows = counts.shape[0]
    row = lax.broadcasted_iota(jnp.int32, (LANES, LANES), 0)
    before = (row < lane_ids((LANES, LANES))).astype(F32)
    inside = lax.dot_general(
        counts, before, NN, precision=exact_mode, preferred_element_type=F32
    )
    totals = jnp.broadcast_to(jnp.sum(counts, axis=1, keepdims=True), counts.shape)
    row = lax.broadcasted_iota(jnp.int32, (rows, rows), 0)
    col = lane_ids((rows, rows))
    earlier = ((col < row) & (col // 8 == row // 8)).astype(F32)
    outside = lax.dot_general(
        earlier, totals, NN, precision=exact_mode, preferred_element_type=F32
    )
    middle = inside + outside + 0.5 * (counts + 1.0)
    level = (middle - 0.375) / (sample_total + 0.25)
    values = math.sqrt(2.0) * erf_inverse(2.0 * level - 1.0)
    place = base_ref[0] + lax.broadcasted_iota(jnp.int32, counts.shape, 0)
    values = jnp.where(place < 736, values, counts)
    for n in range(out_ref.shape[0]):
        out_ref[n] = values


def rank_table(parts, sample_total, base):
    return pl.pallas_call(
        functools.partial(table_kernel, float(sample_total)),
        in_specs=[
            pl.BlockSpec(memory_space=pltpu.SMEM),
            pl.BlockSpec(memory_space=pltpu.VMEM),
        ],
        out_specs=pl.BlockSpec(memory_space=pltpu.VMEM),
        out_shape=jax.ShapeDtypeStruct(parts.shape, F32),
        compiler_params=vmem_params(8),
        name="rank_table",
    )(base, parts)


def lookup(bins, tables):
    lower = bins & 127
    values = [
        jnp.take_along_axis(table, lower, axis=1, mode="promise_in_bounds") for table in tables
    ]
    for bit in (128, 256, 512):
        odd = (bins & bit) != 0
        values = [jnp.where(odd, values[i + 1], values[i]) for i in range(0, len(values), 2)]
    return values[0]


def cross_kernel(
    place_ref, bins_hbm, table_ref, dose_hbm, cov_hbm, plate_hbm, dproj_ref,
    out0_ref, out1_ref, out2_ref, out3_ref, bins_ref, cov_ref, plate_ref, dose_ref, level_ref, total_ref, design_ref, square_ref, sems,
):
    proteins, width = bins_hbm.shape
    chunk = dose_ref.shape[2]
    steps = width // chunk
    spans = [pl.ds(c * chunk, chunk) for c in range(steps)]
    bins_in = [
        pltpu.make_async_copy(
            bins_hbm.at[:, spans[c]], bins_ref.at[c], sems.at[c]
        )
        for c in range(steps)
    ]
    dose_in = [
        pltpu.make_async_copy(dose_hbm.at[:, spans[c]], dose_ref.at[c], sems.at[steps + c])
        for c in range(steps)
    ]
    rest_in = [
        pltpu.make_async_copy(cov_hbm, cov_ref, sems.at[2 * steps]),
        pltpu.make_async_copy(plate_hbm, plate_ref, sems.at[2 * steps + 1]),
    ]
    for copy in [bins_in[0], bins_in[1]] + rest_in + [dose_in[0]] + bins_in[2:] + dose_in[1:]:
        copy.start()
    square_ref[...] = jnp.zeros_like(square_ref)
    for c in range(steps):
        level_ref[c, 96:128, :] = jnp.zeros((32, chunk), BF16)
        level_ref[c, 224:256, :] = jnp.zeros((32, chunk), BF16)

    def levels(c):
        for g in range(0, 12, 2):
            pair = []
            for first in (g, g + 1):
                size = min(8, proteins - 8 * first)
                tables = [table_ref[pl.ds(64 * first + k, size, stride=8), :] for k in range(8)]
                pieces, squares = [], None
                for start in range(0, chunk, LANES):
                    bins = bins_ref[c, 8 * first : 8 * first + size, start : start + LANES]
                    value = lookup(bins, tables)
                    pieces.append(value)
                    squares = value * value if squares is None else squares + value * value
                square_ref[8 * first : 8 * first + size, :] += squares
                pieces = jnp.concatenate(pieces, axis=1)
                if size < 8:
                    pieces = jnp.concatenate([pieces, jnp.zeros((8 - size, chunk), F32)], axis=0)
                pair.append(pieces)
            value = jnp.concatenate(pair, axis=0)
            high = value.astype(BF16)
            low = (value - high.astype(F32)).astype(BF16)
            level_ref[c, 8 * g : 8 * g + 16, :] = high
            level_ref[c, 128 + 8 * g : 128 + 8 * g + 16, :] = low

    bins_in[0].wait()
    levels(0)
    for c in range(steps):
        dose_in[c].wait()
        if c == 0:
            for copy in rest_in:
                copy.wait()
        if c + 1 < steps:
            bins_in[c + 1].wait()
            levels(c + 1)
        level = level_ref[c]
        span = slice(c * chunk, (c + 1) * chunk)
        stack = jnp.concatenate(design_parts(cov_ref[:, span], plate_ref[:, span]), axis=0)
        design = lax.dot_general(stack, level, NT, preferred_element_type=F32)
        total = lax.dot_general(dose_ref[c], level, NT, preferred_element_type=F32)
        if c == 0:
            design_ref[...] = design
            total_ref[...] = total
        else:
            design_ref[...] += design
            total_ref[...] += total
    wide = design_ref[0:64, :] + design_ref[64:128, :] + design_ref[128:192, :]
    proj = wide[:, :LANES] + wide[:, LANES:]
    squares = lax.dot_general(
        jnp.ones((8, LANES), F32), square_ref[...], NT,
        precision=exact_mode, preferred_element_type=F32,
    )
    spare = lane_ids((64, LANES)) >= 96
    own = [pltpu.roll(squares[0:1], shift, 1) for shift in (96, 64, 32)]
    for d, out_ref in enumerate((out0_ref, out1_ref, out2_ref, out3_ref)):
        x = lax.rem(place_ref[1] + d, 4)
        first = pl.multiple_of(256 * x, 256)
        second = pl.multiple_of(256 * x + LANES, LANES)
        rows = total_ref[pl.ds(first, 256), :]
        out_ref[0:256, :] = rows[:, :LANES] + rows[:, LANES:]
        low = dproj_ref[:, pl.ds(first, LANES)]
        high = dproj_ref[:, pl.ds(second, LANES)]
        out_ref[256:320, :] = low[0:64]
        out_ref[320:384, :] = high[0:64]
        dose_own = []
        for z in range(8):
            row = (low, high)[z // 4][64:65]
            dose_own.append(pltpu.roll(row, 96 - 32 * (z % 4), 1) if z % 4 < 3 else row)
        pieces = jnp.concatenate(own + dose_own + [jnp.zeros((53, LANES), F32)], axis=0)
        out_ref[384:448, :] = jnp.where(spare, pieces, proj)


def cross_products(place, bin_ids, table, dosages, covariates, plates, dose_proj):
    count, width = dosages.shape
    chunk = CROSS_CHUNK
    steps = width // chunk
    whole = pl.BlockSpec(memory_space=pltpu.VMEM)
    hbm = pl.BlockSpec(memory_space=pl.ANY)
    return pl.pallas_call(
        cross_kernel,
        in_specs=[pl.BlockSpec(memory_space=pltpu.SMEM), hbm, whole, hbm, hbm, hbm, whole],
        out_specs=[whole] * 4,
        out_shape=[jax.ShapeDtypeStruct((448, LANES), F32)] * 4,
        scratch_shapes=[
            pltpu.VMEM((steps, bin_ids.shape[0], chunk), jnp.int32),
            pltpu.VMEM((COVARS, width), F32),
            pltpu.VMEM((1, width), jnp.int32),
            pltpu.VMEM((steps, count, chunk), BF16),
            pltpu.VMEM((steps, 256, chunk), BF16),
            pltpu.VMEM((count, 256), F32),
            pltpu.VMEM((192, 256), F32),
            pltpu.VMEM((LANES, LANES), F32),
            pltpu.SemaphoreType.DMA((2 * steps + 2,)),
        ],
        compiler_params=vmem_params(50),
        name="cross_products",
    )(place, bin_ids, table, dosages, covariates, plates, dose_proj)


def regroup_kernel(own_ref, first_ref, second_ref, third_ref, out_ref):
    total = own_ref[...] + first_ref[...] + second_ref[...] + third_ref[...]
    proj = total[384:448]
    for z in range(8):
        squares = jnp.concatenate(
            [proj[0:3], proj[3 + z : 4 + z], jnp.zeros((28, LANES), F32)], axis=0
        )
        cross = total[32 * z : 32 * z + 32]
        out_ref[z, 0:32, :] = jnp.where(lane_ids((32, LANES)) >= 96, squares, cross)
        dose = total[256 + 64 * (z // 4) : 320 + 64 * (z // 4)]
        dose = pltpu.roll(dose, 96 - 32 * (z % 4), 1) if z % 4 < 3 else dose
        out_ref[z, 32:96, :] = jnp.where(lane_ids((64, LANES)) >= 96, dose, proj)


def regroup(*parts):
    whole = pl.BlockSpec(memory_space=pltpu.VMEM)
    return pl.pallas_call(
        regroup_kernel,
        in_specs=[whole] * 4,
        out_specs=whole,
        out_shape=jax.ShapeDtypeStruct((8, 96, LANES), F32),
        compiler_params=vmem_params(8),
        name="regroup",
    )(*parts)


def inverse_kernel(gram_ref, out_ref):
    packed = gram_ref[...]
    lane = lane_ids((DESIGN, LANES))
    row = lax.broadcasted_iota(jnp.int32, (DESIGN, LANES), 0)
    work = jnp.concatenate([packed, pltpu.roll(packed, 64, 1)], axis=0)
    work = jnp.where(lane < DESIGN, work, jnp.where(lane == row + DESIGN, 1.0, 0.0))
    plate = work[COVARS:]
    low_lane = lane_ids((PLATES, LANES))
    low_row = lax.broadcasted_iota(jnp.int32, (PLATES, LANES), 0)
    pivots = jnp.sum(
        jnp.where(low_lane == low_row + COVARS, plate, 0.0), axis=1, keepdims=True
    )
    upper = work[:COVARS]
    coupling = upper[:, COVARS:DESIGN]
    upper = upper - lax.dot_general(
        coupling, plate * (1.0 / pivots), NN, precision=exact_mode, preferred_element_type=F32
    )
    for k in range(COVARS):
        first = k // 8 * 8
        source = upper[k : k + 1]
        rest = upper[first:]
        scale = 1.0 / source[:, k : k + 1]
        below = lax.broadcasted_iota(jnp.int32, rest.shape, 0) > k - first
        factor = jnp.where(below, rest[:, k : k + 1] * (source * scale), 0.0)
        rest = rest - factor
        upper = jnp.concatenate([upper[:first], rest], axis=0) if first else rest
    work = jnp.concatenate([upper, plate], axis=0)
    diagonal = jnp.sum(jnp.where(lane == row, work, 0.0), axis=1, keepdims=True)
    out_ref[...] = pltpu.roll(work * lax.rsqrt(diagonal), 64, 1)[:, :DESIGN]


def inverse_factor(table):
    return pl.pallas_call(
        inverse_kernel,
        grid=(1,),
        in_specs=[pl.BlockSpec((32, LANES), lambda i: (23, 0))],
        out_specs=pl.BlockSpec((DESIGN, DESIGN), lambda i: (0, 0)),
        out_shape=jax.ShapeDtypeStruct((DESIGN, DESIGN), F32),
        compiler_params=vmem_params(8),
        cost_estimate=pl.CostEstimate(flops=4_000_000_000, bytes_accessed=32768, transcendentals=0),
        name="inverse_factor",
    )(table)


def finish_kernel(freedom, parts_ref, inverse_ref, out_ref):
    total = parts_ref[0]
    for z in range(1, 8):
        total = total + parts_ref[z]
    shape = (32, LANES)
    lane = lane_ids((1, LANES))
    white = lax.dot_general(
        inverse_ref[...], total[32:96], NN, precision=exact_mode, preferred_element_type=F32
    )
    shared = lax.dot_general(
        white, white, (((0,), (0,)), ((), ())), precision=exact_mode, preferred_element_type=F32
    )
    removed = jnp.sum(white * white, axis=0, keepdims=True)
    expr_sq = [pltpu.roll(total[j : j + 1], 32 * j + 32, 1) for j in range(3)]
    expr_sq = jnp.where(lane < 32, expr_sq[0], jnp.where(lane < 64, expr_sq[1], expr_sq[2]))
    expr_norm = expr_sq - removed
    own = lane_ids(shape) == lax.broadcasted_iota(jnp.int32, shape, 0) + 96
    dose_norm = jnp.broadcast_to(total[3:4] - removed, shape)
    dose_norm = jnp.sum(jnp.where(own, dose_norm, 0.0), axis=1, keepdims=True)
    cross = total[0:32] - shared[96:128]
    corr = cross * lax.rsqrt(dose_norm * expr_norm + tiny_eps)
    stats = corr * jnp.sqrt(freedom / (1.0 - corr * corr))
    out_ref[...] = stats[:, : out_ref.shape[1]]


def finish(parts, inverse, freedom, proteins):
    whole = pl.BlockSpec(memory_space=pltpu.VMEM)
    return pl.pallas_call(
        functools.partial(finish_kernel, float(freedom)),
        in_specs=[whole, whole],
        out_specs=whole,
        out_shape=jax.ShapeDtypeStruct((32, proteins), F32),
        compiler_params=vmem_params(8),
        name="finish",
    )(parts, inverse)


def body(bin_ids, plate_ids, covariates, dosages):
    sample_total = bin_ids.shape[1] * lax.axis_size("samp")
    plates = plate_ids[None, :]
    z_groups = [[x * 8 + z for z in range(8)] for x in range(4)]
    me = lax.axis_index("samp").astype(jnp.int32)
    base = jnp.stack([me * 24, me // 8])

    counts = histogram(bin_ids, covariates, plates).reshape(32, 24, LANES)
    counts = lax.all_to_all(counts, "samp", 0, 0, tiled=True)
    dose_proj = dose_products(dosages, covariates, plates)
    counts, dose_proj = lax.optimization_barrier((counts, dose_proj))
    table = rank_table(counts, sample_total, base)
    table = lax.all_to_all(table, "samp", 0, 0, tiled=True).reshape(768, LANES)
    own, *others = cross_products(
        base, bin_ids, table, dosages, covariates, plates, dose_proj
    )
    late_table, own = lax.optimization_barrier((table, own))
    inverse = inverse_factor(late_table)
    moved = {}
    for d in (2, 1, 3):
        pairs = [(x * 8 + z, (x + d) % 4 * 8 + z) for x in range(4) for z in range(8)]
        moved[d] = lax.ppermute(others[d - 1], "samp", pairs)
    own, inverse = lax.optimization_barrier((own, inverse))
    parts = regroup(own, moved[1], moved[2], moved[3])
    parts = lax.all_to_all(parts, "samp", 0, 0, axis_index_groups=z_groups, tiled=True)
    return finish(parts, inverse, sample_total - DESIGN - 1.0, bin_ids.shape[0])


def solution(mesh):
    placed = (P("prot", "samp"), P("samp"), P(None, "samp"), P(None, "samp"))
    return jax.shard_map(
        body, mesh=mesh, in_specs=placed, out_specs=P("samp", "prot"), check_vma=False
    )
```

```python
import functools
import math

import jax
import jax.numpy as jnp
from jax import lax
from jax.experimental import pallas as pl
from jax.experimental.pallas import tpu as pltpu
from jax.sharding import PartitionSpec as P

BINS = 1024
PLATES = 24
COVARS = 40
DESIGN = 64
DOSE_CHUNK = 1024
CROSS_CHUNK = 1024
LANES = 128
tiny_eps = 1e-06
F32 = jnp.float32
BF16 = jnp.bfloat16
FP8 = jnp.float8_e4m3fn
exact_mode = lax.Precision.HIGHEST
NT = (((1,), (1,)), ((), ()))
NN = (((1,), (0,)), ((), ()))


def vmem_params(mib):
    return pltpu.CompilerParams(vmem_limit_bytes=mib * 1024 * 1024)


def lane_ids(shape):
    return lax.broadcasted_iota(jnp.int32, shape, len(shape) - 1)


def design_parts(cov, plates):
    width = cov.shape[1]
    rows = lax.broadcasted_iota(jnp.int32, (PLATES, width), 0)
    plate_rows = jnp.where(plates == rows, 1.0, 0.0).astype(F32)
    design = jnp.concatenate([cov, plate_rows], axis=0)
    high = design.astype(BF16)
    rest = design - high.astype(F32)
    middle = rest.astype(BF16)
    low = (rest - middle.astype(F32)).astype(BF16)
    return high, middle, low


def fold_lanes(wide):
    first, second = wide[:, :LANES], wide[:, LANES:]
    pair = first + second
    return pair + pltpu.roll(pair, 64, 1)


WAITS = {0: (0, 1), 2: tuple(range(2, 14))}


def hist_kernel(bins_hbm, cov_hbm, plate_hbm, out_ref, bins_ref, cov_ref, plate_ref, table_ref, sems):
    proteins, width = bins_hbm.shape
    chunk = 1024
    groups = [(start, min(8, proteins - start)) for start in range(0, proteins, 8)]
    copies = [
        pltpu.make_async_copy(
            bins_hbm.at[pl.ds(start, size)], bins_ref.at[pl.ds(start, size)], sems.at[n]
        )
        for n, (start, size) in enumerate(groups)
    ]
    copies.append(pltpu.make_async_copy(cov_hbm, cov_ref, sems.at[len(groups)]))
    copies.append(pltpu.make_async_copy(plate_hbm, plate_ref, sems.at[len(groups) + 1]))
    for copy in copies:
        copy.start()
    ids = lax.broadcasted_iota(jnp.int32, (32, chunk), 0).astype(jnp.int8)
    one = jnp.ones((32, chunk), F32).astype(FP8)
    zero = jnp.zeros((32, chunk), F32).astype(FP8)
    block = lane_ids((8, LANES)) // 32
    for n, (first, size) in enumerate(groups):
        for k in WAITS.get(n, ()):
            copies[k].wait()
        side = 32 * size
        total = jnp.zeros((side, side), F32)
        for start in range(0, width, chunk):
            bins = bins_ref[first : first + size, start : start + chunk]
            left, right = [], []
            for p in range(size):
                row = jnp.broadcast_to(bins[p : p + 1], (32, chunk))
                left.append(jnp.where((row >> 5).astype(jnp.int8) == ids, one, zero))
                right.append(jnp.where((row & 31).astype(jnp.int8) == ids, one, zero))
            total = total + lax.dot_general(
                jnp.concatenate(left, axis=0),
                jnp.concatenate(right, axis=0),
                NT,
                preferred_element_type=F32,
            )
        lane = lane_ids((32, side)) // 32
        diag = total[:32]
        for p in range(1, size):
            diag = jnp.where(lane == p, total[32 * p : 32 * p + 32], diag)
        for half in range(side // LANES):
            table_ref[n % 2, half] = diag[:, half * LANES : (half + 1) * LANES]
            rows = [table_ref[n % 2, half, pl.ds(c, 8, stride=4), :] for c in range(4)]
            for q in range(4):
                out = rows[q]
                for c in range(4):
                    shift = ((c - q) % 4) * 32
                    moved = pltpu.roll(rows[c], shift, 1) if shift else rows[c]
                    out = jnp.where(block == c, moved, out)
                p = first + half * 4 + q
                out_ref[8 * p : 8 * p + 8, :] = out
    high, middle, low = design_parts(cov_ref[...], plate_ref[...])
    stack = jnp.concatenate([high, middle, low, jnp.zeros_like(high)], axis=0)
    wide = lax.dot_general(stack[:192], stack, NT, preferred_element_type=F32)
    gram = fold_lanes(wide[:64] + wide[64:128] + wide[128:192])
    out_ref[8 * proteins :, :] = jnp.where(lane_ids((32, LANES)) < 64, gram[:32], gram[32:])


def histogram(bin_ids, covariates, plates):
    proteins, width = bin_ids.shape
    hbm = pl.BlockSpec(memory_space=pl.ANY)
    return pl.pallas_call(
        hist_kernel,
        in_specs=[hbm, hbm, hbm],
        out_specs=pl.BlockSpec(memory_space=pltpu.VMEM),
        out_shape=jax.ShapeDtypeStruct((768, LANES), F32),
        scratch_shapes=[
            pltpu.VMEM((96, width), jnp.int32),
            pltpu.VMEM((COVARS, width), F32),
            pltpu.VMEM((1, width), jnp.int32),
            pltpu.VMEM((2, 2, 32, LANES), F32),
            pltpu.SemaphoreType.DMA((14,)),
        ],
        compiler_params=vmem_params(60),
        name="histogram",
    )(bin_ids, covariates, plates)


def dose_kernel(dose_hbm, cov_ref, plate_ref, proj_ref, dose_ref, total_ref, part_ref, sems):
    chunk = dose_ref.shape[2]
    copies = [
        pltpu.make_async_copy(
            dose_hbm.at[:, pl.ds(c * chunk, chunk)], dose_ref.at[c], sems.at[c]
        )
        for c in range(dose_ref.shape[0])
    ]
    for copy in copies:
        copy.start()
    high, middle, low = design_parts(cov_ref[...], plate_ref[...])
    stack = jnp.concatenate([high, middle, low, jnp.zeros_like(high)], axis=0)
    for c in range(len(copies)):
        copies[c].wait()
        for r in range(0, dose_ref.shape[1], 256):
            dose = dose_ref[c, r : r + 256, :]
            term = lax.dot_general(
                dose, stack[:, c * chunk : (c + 1) * chunk], NT, preferred_element_type=F32
            )
            wide = dose.astype(F32)
            wide = wide * wide
            part = wide[:, :LANES]
            for start in range(LANES, chunk, LANES):
                part = part + wide[:, start : start + LANES]
            if c == 0:
                total_ref[r : r + 256, :] = term
                part_ref[r : r + 256, :] = part
            else:
                total_ref[r : r + 256, :] += term
                part_ref[r : r + 256, :] += part
    for c in range(proj_ref.shape[1] // LANES):
        span = slice(LANES * c, LANES * (c + 1))
        proj_ref[0:64, span] = fold_lanes(total_ref[span, :]).T[:64]
    squares = lax.dot_general(
        jnp.ones((8, LANES), F32), part_ref[...], NT,
        precision=exact_mode, preferred_element_type=F32,
    )
    proj_ref[64:72, :] = squares


def dose_products(dosages, covariates, plates):
    count, width = dosages.shape
    chunk = DOSE_CHUNK
    whole = pl.BlockSpec(memory_space=pltpu.VMEM)
    return pl.pallas_call(
        dose_kernel,
        in_specs=[pl.BlockSpec(memory_space=pl.ANY), whole, whole],
        out_specs=whole,
        out_shape=jax.ShapeDtypeStruct((DESIGN + 8, count), F32),
        scratch_shapes=[
            pltpu.VMEM((width // chunk, count, chunk), BF16),
            pltpu.VMEM((count, 256), F32),
            pltpu.VMEM((count, LANES), F32),
            pltpu.SemaphoreType.DMA((width // chunk,)),
        ],
        compiler_params=vmem_params(50),
        cost_estimate=pl.CostEstimate(
            flops=2 * count * width * 256, bytes_accessed=count * width * 2, transcendentals=0
        ),
        name="dose_products",
    )(dosages, covariates, plates)


def erf_inverse(x):
    w = -jnp.log1p(-x * x)
    small = w < 5.0
    shifted = jnp.where(small, w - 2.5, jnp.sqrt(w) - 3.0)
    near = (
        2.81022636e-08, 3.43273939e-07, -3.5233877e-06, -4.39150654e-06, 0.00021858087,
        -0.00125372503, -0.00417768164, 0.246640727, 1.50140941,
    )
    far = (
        -0.000200214257, 0.000100950558, 0.00134934322, -0.00367342844, 0.00573950773,
        -0.0076224613, 0.00943887047, 1.00167406, 2.83297682,
    )
    value = jnp.where(small, near[0], far[0])
    for a, b in zip(near[1:], far[1:]):
        value = value * shifted + jnp.where(small, a, b)
    return value * x


def table_kernel(sample_total, parts_ref, out_ref):
    counts = jnp.sum(parts_ref[...], axis=0)
    rows = counts.shape[0]
    row = lax.broadcasted_iota(jnp.int32, (LANES, LANES), 0)
    before = (row < lane_ids((LANES, LANES))).astype(F32)
    inside = lax.dot_general(
        counts, before, NN, precision=exact_mode, preferred_element_type=F32
    )
    totals = jnp.broadcast_to(jnp.sum(counts, axis=1, keepdims=True), counts.shape)
    row = lax.broadcasted_iota(jnp.int32, (rows, rows), 0)
    col = lane_ids((rows, rows))
    earlier = ((col < row) & (col // 8 == row // 8)).astype(F32)
    outside = lax.dot_general(
        earlier, totals, NN, precision=exact_mode, preferred_element_type=F32
    )
    middle = inside + outside + 0.5 * (counts + 1.0)
    level = (middle - 0.375) / (sample_total + 0.25)
    values = math.sqrt(2.0) * erf_inverse(2.0 * level - 1.0)
    place = lax.axis_index("samp") * rows + lax.broadcasted_iota(jnp.int32, counts.shape, 0)
    values = jnp.where(place < 736, values, counts)
    for n in range(out_ref.shape[0]):
        out_ref[n] = values


def rank_table(parts, sample_total):
    return pl.pallas_call(
        functools.partial(table_kernel, float(sample_total)),
        in_specs=[pl.BlockSpec(memory_space=pltpu.VMEM)],
        out_specs=pl.BlockSpec(memory_space=pltpu.VMEM),
        out_shape=jax.ShapeDtypeStruct(parts.shape, F32),
        compiler_params=vmem_params(8),
        name="rank_table",
    )(parts)


def lookup(bins, tables):
    lower = bins & 127
    values = [
        jnp.take_along_axis(table, lower, axis=1, mode="promise_in_bounds") for table in tables
    ]
    for bit in (128, 256, 512):
        odd = (bins & bit) != 0
        values = [jnp.where(odd, values[i + 1], values[i]) for i in range(0, len(values), 2)]
    return values[0]


def cross_kernel(
    bins_hbm, table_ref, dose_hbm, cov_hbm, plate_hbm, dproj_ref,
    out0_ref, out1_ref, out2_ref, out3_ref, bins_ref, cov_ref, plate_ref, dose_ref, level_ref, total_ref, design_ref, square_ref, sems,
):
    proteins, width = bins_hbm.shape
    chunk = dose_ref.shape[2]
    steps = width // chunk
    spans = [pl.ds(c * chunk, chunk) for c in range(steps)]
    bins_in = [
        pltpu.make_async_copy(
            bins_hbm.at[:, spans[c]], bins_ref.at[c], sems.at[c]
        )
        for c in range(steps)
    ]
    dose_in = [
        pltpu.make_async_copy(dose_hbm.at[:, spans[c]], dose_ref.at[c], sems.at[steps + c])
        for c in range(steps)
    ]
    rest_in = [
        pltpu.make_async_copy(cov_hbm, cov_ref, sems.at[2 * steps]),
        pltpu.make_async_copy(plate_hbm, plate_ref, sems.at[2 * steps + 1]),
    ]
    for copy in [bins_in[0], bins_in[1]] + rest_in + [dose_in[0]] + bins_in[2:] + dose_in[1:]:
        copy.start()
    square_ref[...] = jnp.zeros_like(square_ref)
    for c in range(steps):
        level_ref[c, 96:128, :] = jnp.zeros((32, chunk), BF16)
        level_ref[c, 224:256, :] = jnp.zeros((32, chunk), BF16)

    def levels(c):
        for g in range(0, 12, 2):
            pair = []
            for first in (g, g + 1):
                size = min(8, proteins - 8 * first)
                tables = [table_ref[pl.ds(64 * first + k, size, stride=8), :] for k in range(8)]
                pieces, squares = [], None
                for start in range(0, chunk, LANES):
                    bins = bins_ref[c, 8 * first : 8 * first + size, start : start + LANES]
                    value = lookup(bins, tables)
                    pieces.append(value)
                    squares = value * value if squares is None else squares + value * value
                square_ref[8 * first : 8 * first + size, :] += squares
                pieces = jnp.concatenate(pieces, axis=1)
                if size < 8:
                    pieces = jnp.concatenate([pieces, jnp.zeros((8 - size, chunk), F32)], axis=0)
                pair.append(pieces)
            value = jnp.concatenate(pair, axis=0)
            high = value.astype(BF16)
            low = (value - high.astype(F32)).astype(BF16)
            level_ref[c, 8 * g : 8 * g + 16, :] = high
            level_ref[c, 128 + 8 * g : 128 + 8 * g + 16, :] = low

    bins_in[0].wait()
    levels(0)
    for c in range(steps):
        dose_in[c].wait()
        if c == 0:
            for copy in rest_in:
                copy.wait()
        if c + 1 < steps:
            bins_in[c + 1].wait()
            levels(c + 1)
        level = level_ref[c]
        span = slice(c * chunk, (c + 1) * chunk)
        stack = jnp.concatenate(design_parts(cov_ref[:, span], plate_ref[:, span]), axis=0)
        design = lax.dot_general(stack, level, NT, preferred_element_type=F32)
        total = lax.dot_general(dose_ref[c], level, NT, preferred_element_type=F32)
        if c == 0:
            design_ref[...] = design
            total_ref[...] = total
        else:
            design_ref[...] += design
            total_ref[...] += total
    wide = design_ref[0:64, :] + design_ref[64:128, :] + design_ref[128:192, :]
    proj = wide[:, :LANES] + wide[:, LANES:]
    squares = lax.dot_general(
        jnp.ones((8, LANES), F32), square_ref[...], NT,
        precision=exact_mode, preferred_element_type=F32,
    )
    spare = lane_ids((64, LANES)) >= 96
    own = [pltpu.roll(squares[0:1], shift, 1) for shift in (96, 64, 32)]
    for d, out_ref in enumerate((out0_ref, out1_ref, out2_ref, out3_ref)):
        x = lax.rem(lax.axis_index("samp") // 8 + d, 4)
        first = pl.multiple_of(256 * x, 256)
        second = pl.multiple_of(256 * x + LANES, LANES)
        rows = total_ref[pl.ds(first, 256), :]
        out_ref[0:256, :] = rows[:, :LANES] + rows[:, LANES:]
        low = dproj_ref[:, pl.ds(first, LANES)]
        high = dproj_ref[:, pl.ds(second, LANES)]
        out_ref[256:320, :] = low[0:64]
        out_ref[320:384, :] = high[0:64]
        dose_own = []
        for z in range(8):
            row = (low, high)[z // 4][64:65]
            dose_own.append(pltpu.roll(row, 96 - 32 * (z % 4), 1) if z % 4 < 3 else row)
        pieces = jnp.concatenate(own + dose_own + [jnp.zeros((53, LANES), F32)], axis=0)
        out_ref[384:448, :] = jnp.where(spare, pieces, proj)


def cross_products(bin_ids, table, dosages, covariates, plates, dose_proj):
    count, width = dosages.shape
    chunk = CROSS_CHUNK
    steps = width // chunk
    whole = pl.BlockSpec(memory_space=pltpu.VMEM)
    hbm = pl.BlockSpec(memory_space=pl.ANY)
    return pl.pallas_call(
        cross_kernel,
        in_specs=[hbm, whole, hbm, hbm, hbm, whole],
        out_specs=[whole] * 4,
        out_shape=[jax.ShapeDtypeStruct((448, LANES), F32)] * 4,
        scratch_shapes=[
            pltpu.VMEM((steps, bin_ids.shape[0], chunk), jnp.int32),
            pltpu.VMEM((COVARS, width), F32),
            pltpu.VMEM((1, width), jnp.int32),
            pltpu.VMEM((steps, count, chunk), BF16),
            pltpu.VMEM((steps, 256, chunk), BF16),
            pltpu.VMEM((count, 256), F32),
            pltpu.VMEM((192, 256), F32),
            pltpu.VMEM((LANES, LANES), F32),
            pltpu.SemaphoreType.DMA((2 * steps + 2,)),
        ],
        compiler_params=vmem_params(50),
        name="cross_products",
    )(bin_ids, table, dosages, covariates, plates, dose_proj)


def regroup_kernel(own_ref, first_ref, second_ref, third_ref, out_ref):
    total = own_ref[...] + first_ref[...] + second_ref[...] + third_ref[...]
    proj = total[384:448]
    for z in range(8):
        squares = jnp.concatenate(
            [proj[0:3], proj[3 + z : 4 + z], jnp.zeros((28, LANES), F32)], axis=0
        )
        cross = total[32 * z : 32 * z + 32]
        out_ref[z, 0:32, :] = jnp.where(lane_ids((32, LANES)) >= 96, squares, cross)
        dose = total[256 + 64 * (z // 4) : 320 + 64 * (z // 4)]
        dose = pltpu.roll(dose, 96 - 32 * (z % 4), 1) if z % 4 < 3 else dose
        out_ref[z, 32:96, :] = jnp.where(lane_ids((64, LANES)) >= 96, dose, proj)


def regroup(*parts):
    whole = pl.BlockSpec(memory_space=pltpu.VMEM)
    return pl.pallas_call(
        regroup_kernel,
        in_specs=[whole] * 4,
        out_specs=whole,
        out_shape=jax.ShapeDtypeStruct((8, 96, LANES), F32),
        compiler_params=vmem_params(8),
        name="regroup",
    )(*parts)


def inverse_kernel(gram_ref, out_ref):
    packed = gram_ref[...]
    lane = lane_ids((DESIGN, LANES))
    row = lax.broadcasted_iota(jnp.int32, (DESIGN, LANES), 0)
    work = jnp.concatenate([packed, pltpu.roll(packed, 64, 1)], axis=0)
    work = jnp.where(lane < DESIGN, work, jnp.where(lane == row + DESIGN, 1.0, 0.0))
    plate = work[COVARS:]
    low_lane = lane_ids((PLATES, LANES))
    low_row = lax.broadcasted_iota(jnp.int32, (PLATES, LANES), 0)
    pivots = jnp.sum(
        jnp.where(low_lane == low_row + COVARS, plate, 0.0), axis=1, keepdims=True
    )
    upper = work[:COVARS]
    coupling = upper[:, COVARS:DESIGN]
    upper = upper - lax.dot_general(
        coupling, plate * (1.0 / pivots), NN, precision=exact_mode, preferred_element_type=F32
    )
    for k in range(COVARS):
        first = k // 8 * 8
        source = upper[k : k + 1]
        rest = upper[first:]
        scale = 1.0 / source[:, k : k + 1]
        below = lax.broadcasted_iota(jnp.int32, rest.shape, 0) > k - first
        factor = jnp.where(below, rest[:, k : k + 1] * (source * scale), 0.0)
        rest = rest - factor
        upper = jnp.concatenate([upper[:first], rest], axis=0) if first else rest
    work = jnp.concatenate([upper, plate], axis=0)
    diagonal = jnp.sum(jnp.where(lane == row, work, 0.0), axis=1, keepdims=True)
    out_ref[...] = pltpu.roll(work * lax.rsqrt(diagonal), 64, 1)[:, :DESIGN]


def inverse_factor(table):
    return pl.pallas_call(
        inverse_kernel,
        grid=(1,),
        in_specs=[pl.BlockSpec((32, LANES), lambda i: (23, 0))],
        out_specs=pl.BlockSpec((DESIGN, DESIGN), lambda i: (0, 0)),
        out_shape=jax.ShapeDtypeStruct((DESIGN, DESIGN), F32),
        compiler_params=vmem_params(8),
        cost_estimate=pl.CostEstimate(flops=4_000_000_000, bytes_accessed=32768, transcendentals=0),
        name="inverse_factor",
    )(table)


def finish_kernel(freedom, parts_ref, inverse_ref, out_ref):
    total = parts_ref[0]
    for z in range(1, 8):
        total = total + parts_ref[z]
    shape = (32, LANES)
    lane = lane_ids((1, LANES))
    white = lax.dot_general(
        inverse_ref[...], total[32:96], NN, precision=exact_mode, preferred_element_type=F32
    )
    shared = lax.dot_general(
        white, white, (((0,), (0,)), ((), ())), precision=exact_mode, preferred_element_type=F32
    )
    removed = jnp.sum(white * white, axis=0, keepdims=True)
    expr_sq = [pltpu.roll(total[j : j + 1], 32 * j + 32, 1) for j in range(3)]
    expr_sq = jnp.where(lane < 32, expr_sq[0], jnp.where(lane < 64, expr_sq[1], expr_sq[2]))
    expr_norm = expr_sq - removed
    own = lane_ids(shape) == lax.broadcasted_iota(jnp.int32, shape, 0) + 96
    dose_norm = jnp.broadcast_to(total[3:4] - removed, shape)
    dose_norm = jnp.sum(jnp.where(own, dose_norm, 0.0), axis=1, keepdims=True)
    cross = total[0:32] - shared[96:128]
    corr = cross * lax.rsqrt(dose_norm * expr_norm + tiny_eps)
    stats = corr * jnp.sqrt(freedom / (1.0 - corr * corr))
    out_ref[...] = stats[:, : out_ref.shape[1]]


def finish(parts, inverse, freedom, proteins):
    whole = pl.BlockSpec(memory_space=pltpu.VMEM)
    return pl.pallas_call(
        functools.partial(finish_kernel, float(freedom)),
        in_specs=[whole, whole],
        out_specs=whole,
        out_shape=jax.ShapeDtypeStruct((32, proteins), F32),
        compiler_params=vmem_params(8),
        name="finish",
    )(parts, inverse)


def body(bin_ids, plate_ids, covariates, dosages):
    sample_total = bin_ids.shape[1] * lax.axis_size("samp")
    plates = plate_ids[None, :]
    z_groups = [[x * 8 + z for z in range(8)] for x in range(4)]

    counts = histogram(bin_ids, covariates, plates).reshape(32, 24, LANES)
    counts = lax.all_to_all(counts, "samp", 0, 0, tiled=True)
    dose_proj = dose_products(dosages, covariates, plates)
    counts, dose_proj = lax.optimization_barrier((counts, dose_proj))
    table = rank_table(counts, sample_total)
    table = lax.all_to_all(table, "samp", 0, 0, tiled=True).reshape(768, LANES)
    own, *others = cross_products(
        bin_ids, table, dosages, covariates, plates, dose_proj
    )
    late_table, own = lax.optimization_barrier((table, own))
    inverse = inverse_factor(late_table)
    moved = {}
    for d in (2, 1, 3):
        pairs = [(x * 8 + z, (x + d) % 4 * 8 + z) for x in range(4) for z in range(8)]
        moved[d] = lax.ppermute(others[d - 1], "samp", pairs)
    own, inverse = lax.optimization_barrier((own, inverse))
    parts = regroup(own, moved[1], moved[2], moved[3])
    parts = lax.all_to_all(parts, "samp", 0, 0, axis_index_groups=z_groups, tiled=True)
    return finish(parts, inverse, sample_total - DESIGN - 1.0, bin_ids.shape[0])


def solution(mesh):
    placed = (P("prot", "samp"), P("samp"), P(None, "samp"), P(None, "samp"))
    return jax.shard_map(
        body, mesh=mesh, in_specs=placed, out_specs=P("samp", "prot"), check_vma=False
    )
```

```python
import functools
import math

import jax
import jax.numpy as jnp
from jax import lax
from jax.experimental import pallas as pl
from jax.experimental.pallas import tpu as pltpu
from jax.sharding import PartitionSpec as P

BINS = 1024
PLATES = 24
COVARS = 40
DESIGN = 64
DOSE_CHUNK = 1024
CROSS_CHUNK = 1024
LANES = 128
tiny_eps = 1e-06
F32 = jnp.float32
BF16 = jnp.bfloat16
FP8 = jnp.float8_e4m3fn
exact_mode = lax.Precision.HIGHEST
NT = (((1,), (1,)), ((), ()))
NN = (((1,), (0,)), ((), ()))


def vmem_params(mib):
    return pltpu.CompilerParams(vmem_limit_bytes=mib * 1024 * 1024)


def lane_ids(shape):
    return lax.broadcasted_iota(jnp.int32, shape, len(shape) - 1)


def design_parts(cov, plates):
    width = cov.shape[1]
    rows = lax.broadcasted_iota(jnp.int32, (PLATES, width), 0)
    plate_rows = jnp.where(plates == rows, 1.0, 0.0).astype(F32)
    design = jnp.concatenate([cov, plate_rows], axis=0)
    high = design.astype(BF16)
    rest = design - high.astype(F32)
    middle = rest.astype(BF16)
    low = (rest - middle.astype(F32)).astype(BF16)
    return high, middle, low


def fold_lanes(wide):
    first, second = wide[:, :LANES], wide[:, LANES:]
    pair = first + second
    return pair + pltpu.roll(pair, 64, 1)


WAITS = {0: (0, 1), 2: tuple(range(2, 14))}


def hist_kernel(bins_hbm, cov_hbm, plate_hbm, out_ref, bins_ref, cov_ref, plate_ref, table_ref, sems):
    proteins, width = bins_hbm.shape
    chunk = 1024
    groups = [(start, min(8, proteins - start)) for start in range(0, proteins, 8)]
    copies = [
        pltpu.make_async_copy(
            bins_hbm.at[pl.ds(start, size)], bins_ref.at[pl.ds(start, size)], sems.at[n]
        )
        for n, (start, size) in enumerate(groups)
    ]
    copies.append(pltpu.make_async_copy(cov_hbm, cov_ref, sems.at[len(groups)]))
    copies.append(pltpu.make_async_copy(plate_hbm, plate_ref, sems.at[len(groups) + 1]))
    for copy in copies:
        copy.start()
    ids = lax.broadcasted_iota(jnp.int32, (32, chunk), 0).astype(jnp.int8)
    one = jnp.ones((32, chunk), F32).astype(FP8)
    zero = jnp.zeros((32, chunk), F32).astype(FP8)
    block = lane_ids((8, LANES)) // 32
    for n, (first, size) in enumerate(groups):
        for k in WAITS.get(n, ()):
            copies[k].wait()
        side = 32 * size
        total = jnp.zeros((side, side), F32)
        for start in range(0, width, chunk):
            bins = bins_ref[first : first + size, start : start + chunk]
            left, right = [], []
            for p in range(size):
                row = jnp.broadcast_to(bins[p : p + 1], (32, chunk))
                left.append(jnp.where((row >> 5).astype(jnp.int8) == ids, one, zero))
                right.append(jnp.where((row & 31).astype(jnp.int8) == ids, one, zero))
            total = total + lax.dot_general(
                jnp.concatenate(left, axis=0),
                jnp.concatenate(right, axis=0),
                NT,
                preferred_element_type=F32,
            )
        lane = lane_ids((32, side)) // 32
        diag = total[:32]
        for p in range(1, size):
            diag = jnp.where(lane == p, total[32 * p : 32 * p + 32], diag)
        for half in range(side // LANES):
            table_ref[n % 2, half] = diag[:, half * LANES : (half + 1) * LANES]
            rows = [table_ref[n % 2, half, pl.ds(c, 8, stride=4), :] for c in range(4)]
            for q in range(4):
                out = rows[q]
                for c in range(4):
                    shift = ((c - q) % 4) * 32
                    moved = pltpu.roll(rows[c], shift, 1) if shift else rows[c]
                    out = jnp.where(block == c, moved, out)
                p = first + half * 4 + q
                out_ref[8 * p : 8 * p + 8, :] = out
    high, middle, low = design_parts(cov_ref[...], plate_ref[...])
    stack = jnp.concatenate([high, middle, low, jnp.zeros_like(high)], axis=0)
    wide = lax.dot_general(stack[:192], stack, NT, preferred_element_type=F32)
    gram = fold_lanes(wide[:64] + wide[64:128] + wide[128:192])
    out_ref[8 * proteins :, :] = jnp.where(lane_ids((32, LANES)) < 64, gram[:32], gram[32:])


def histogram(bin_ids, covariates, plates):
    proteins, width = bin_ids.shape
    hbm = pl.BlockSpec(memory_space=pl.ANY)
    return pl.pallas_call(
        hist_kernel,
        in_specs=[hbm, hbm, hbm],
        out_specs=pl.BlockSpec(memory_space=pltpu.VMEM),
        out_shape=jax.ShapeDtypeStruct((768, LANES), F32),
        scratch_shapes=[
            pltpu.VMEM((96, width), jnp.int32),
            pltpu.VMEM((COVARS, width), F32),
            pltpu.VMEM((1, width), jnp.int32),
            pltpu.VMEM((2, 2, 32, LANES), F32),
            pltpu.SemaphoreType.DMA((14,)),
        ],
        compiler_params=vmem_params(60),
        name="histogram",
    )(bin_ids, covariates, plates)


def dose_kernel(dose_hbm, cov_ref, plate_ref, proj_ref, dose_ref, total_ref, part_ref, sems):
    chunk = dose_ref.shape[2]
    copies = [
        pltpu.make_async_copy(
            dose_hbm.at[:, pl.ds(c * chunk, chunk)], dose_ref.at[c], sems.at[c]
        )
        for c in range(dose_ref.shape[0])
    ]
    for copy in copies:
        copy.start()
    high, middle, low = design_parts(cov_ref[...], plate_ref[...])
    stack = jnp.concatenate([high, middle, low, jnp.zeros_like(high)], axis=0)
    for c in range(len(copies)):
        copies[c].wait()
        for r in range(0, dose_ref.shape[1], 256):
            dose = dose_ref[c, r : r + 256, :]
            term = lax.dot_general(
                dose, stack[:, c * chunk : (c + 1) * chunk], NT, preferred_element_type=F32
            )
            wide = dose.astype(F32)
            wide = wide * wide
            part = wide[:, :LANES]
            for start in range(LANES, chunk, LANES):
                part = part + wide[:, start : start + LANES]
            if c == 0:
                total_ref[r : r + 256, :] = term
                part_ref[r : r + 256, :] = part
            else:
                total_ref[r : r + 256, :] += term
                part_ref[r : r + 256, :] += part
    for c in range(proj_ref.shape[1] // LANES):
        span = slice(LANES * c, LANES * (c + 1))
        proj_ref[0:64, span] = fold_lanes(total_ref[span, :]).T[:64]
    squares = lax.dot_general(
        jnp.ones((8, LANES), F32), part_ref[...], NT,
        precision=exact_mode, preferred_element_type=F32,
    )
    proj_ref[64:72, :] = squares


def dose_products(dosages, covariates, plates):
    count, width = dosages.shape
    chunk = DOSE_CHUNK
    whole = pl.BlockSpec(memory_space=pltpu.VMEM)
    return pl.pallas_call(
        dose_kernel,
        in_specs=[pl.BlockSpec(memory_space=pl.ANY), whole, whole],
        out_specs=whole,
        out_shape=jax.ShapeDtypeStruct((DESIGN + 8, count), F32),
        scratch_shapes=[
            pltpu.VMEM((width // chunk, count, chunk), BF16),
            pltpu.VMEM((count, 256), F32),
            pltpu.VMEM((count, LANES), F32),
            pltpu.SemaphoreType.DMA((width // chunk,)),
        ],
        compiler_params=vmem_params(50),
        cost_estimate=pl.CostEstimate(
            flops=2 * count * width * 256, bytes_accessed=count * width * 2, transcendentals=0
        ),
        name="dose_products",
    )(dosages, covariates, plates)


def erf_inverse(x):
    w = -jnp.log1p(-x * x)
    small = w < 5.0
    shifted = jnp.where(small, w - 2.5, jnp.sqrt(w) - 3.0)
    near = (
        2.81022636e-08, 3.43273939e-07, -3.5233877e-06, -4.39150654e-06, 0.00021858087,
        -0.00125372503, -0.00417768164, 0.246640727, 1.50140941,
    )
    far = (
        -0.000200214257, 0.000100950558, 0.00134934322, -0.00367342844, 0.00573950773,
        -0.0076224613, 0.00943887047, 1.00167406, 2.83297682,
    )
    value = jnp.where(small, near[0], far[0])
    for a, b in zip(near[1:], far[1:]):
        value = value * shifted + jnp.where(small, a, b)
    return value * x


def table_kernel(sample_total, parts_ref, out_ref):
    counts = jnp.sum(parts_ref[...], axis=0)
    rows = counts.shape[0]
    row = lax.broadcasted_iota(jnp.int32, (LANES, LANES), 0)
    before = (row < lane_ids((LANES, LANES))).astype(F32)
    inside = lax.dot_general(
        counts, before, NN, precision=exact_mode, preferred_element_type=F32
    )
    totals = jnp.broadcast_to(jnp.sum(counts, axis=1, keepdims=True), counts.shape)
    row = lax.broadcasted_iota(jnp.int32, (rows, rows), 0)
    col = lane_ids((rows, rows))
    earlier = ((col < row) & (col // 8 == row // 8)).astype(F32)
    outside = lax.dot_general(
        earlier, totals, NN, precision=exact_mode, preferred_element_type=F32
    )
    middle = inside + outside + 0.5 * (counts + 1.0)
    level = (middle - 0.375) / (sample_total + 0.25)
    values = math.sqrt(2.0) * erf_inverse(2.0 * level - 1.0)
    place = lax.axis_index("samp") * rows + lax.broadcasted_iota(jnp.int32, counts.shape, 0)
    values = jnp.where(place < 736, values, counts)
    for n in range(out_ref.shape[0]):
        out_ref[n] = values


def rank_table(parts, sample_total):
    return pl.pallas_call(
        functools.partial(table_kernel, float(sample_total)),
        in_specs=[pl.BlockSpec(memory_space=pltpu.VMEM)],
        out_specs=pl.BlockSpec(memory_space=pltpu.VMEM),
        out_shape=jax.ShapeDtypeStruct(parts.shape, F32),
        compiler_params=vmem_params(8),
        name="rank_table",
    )(parts)


def lookup(bins, tables):
    lower = bins & 127
    values = [
        jnp.take_along_axis(table, lower, axis=1, mode="promise_in_bounds") for table in tables
    ]
    for bit in (128, 256, 512):
        odd = (bins & bit) != 0
        values = [jnp.where(odd, values[i + 1], values[i]) for i in range(0, len(values), 2)]
    return values[0]


def cross_kernel(
    bins_hbm, table_ref, dose_hbm, cov_hbm, plate_hbm, dproj_ref,
    out0_ref, out1_ref, out2_ref, out3_ref, bins_ref, cov_ref, plate_ref, dose_ref, level_ref, total_ref, design_ref, square_ref, sems,
):
    proteins, width = bins_hbm.shape
    chunk = dose_ref.shape[2]
    steps = width // chunk
    spans = [pl.ds(c * chunk, chunk) for c in range(steps)]
    bins_in = [
        pltpu.make_async_copy(
            bins_hbm.at[:, spans[c]], bins_ref.at[c], sems.at[c]
        )
        for c in range(steps)
    ]
    dose_in = [
        pltpu.make_async_copy(dose_hbm.at[:, spans[c]], dose_ref.at[c], sems.at[steps + c])
        for c in range(steps)
    ]
    rest_in = [
        pltpu.make_async_copy(cov_hbm, cov_ref, sems.at[2 * steps]),
        pltpu.make_async_copy(plate_hbm, plate_ref, sems.at[2 * steps + 1]),
    ]
    for copy in [bins_in[0], bins_in[1]] + rest_in + [dose_in[0]] + bins_in[2:] + dose_in[1:]:
        copy.start()
    square_ref[...] = jnp.zeros_like(square_ref)
    for c in range(steps):
        level_ref[c, 96:128, :] = jnp.zeros((32, chunk), BF16)
        level_ref[c, 224:256, :] = jnp.zeros((32, chunk), BF16)

    def levels(c):
        for g in range(0, 12, 2):
            pair = []
            for first in (g, g + 1):
                size = min(8, proteins - 8 * first)
                tables = [table_ref[pl.ds(64 * first + k, size, stride=8), :] for k in range(8)]
                pieces, squares = [], None
                for start in range(0, chunk, LANES):
                    bins = bins_ref[c, 8 * first : 8 * first + size, start : start + LANES]
                    value = lookup(bins, tables)
                    pieces.append(value)
                    squares = value * value if squares is None else squares + value * value
                square_ref[8 * first : 8 * first + size, :] += squares
                pieces = jnp.concatenate(pieces, axis=1)
                if size < 8:
                    pieces = jnp.concatenate([pieces, jnp.zeros((8 - size, chunk), F32)], axis=0)
                pair.append(pieces)
            value = jnp.concatenate(pair, axis=0)
            high = value.astype(BF16)
            low = (value - high.astype(F32)).astype(BF16)
            level_ref[c, 8 * g : 8 * g + 16, :] = high
            level_ref[c, 128 + 8 * g : 128 + 8 * g + 16, :] = low

    bins_in[0].wait()
    levels(0)
    for c in range(steps):
        dose_in[c].wait()
        if c == 0:
            for copy in rest_in:
                copy.wait()
        if c + 1 < steps:
            bins_in[c + 1].wait()
            levels(c + 1)
        level = level_ref[c]
        span = slice(c * chunk, (c + 1) * chunk)
        stack = jnp.concatenate(design_parts(cov_ref[:, span], plate_ref[:, span]), axis=0)
        design = lax.dot_general(stack, level, NT, preferred_element_type=F32)
        total = lax.dot_general(dose_ref[c], level, NT, preferred_element_type=F32)
        if c == 0:
            design_ref[...] = design
            total_ref[...] = total
        else:
            design_ref[...] += design
            total_ref[...] += total
    wide = design_ref[0:64, :] + design_ref[64:128, :] + design_ref[128:192, :]
    proj = wide[:, :LANES] + wide[:, LANES:]
    squares = lax.dot_general(
        jnp.ones((8, LANES), F32), square_ref[...], NT,
        precision=exact_mode, preferred_element_type=F32,
    )
    spare = lane_ids((64, LANES)) >= 96
    own = [pltpu.roll(squares[0:1], shift, 1) for shift in (96, 64, 32)]
    for d, out_ref in enumerate((out0_ref, out1_ref, out2_ref, out3_ref)):
        x = lax.rem(lax.axis_index("samp") // 8 + d, 4)
        first = pl.multiple_of(256 * x, 256)
        second = pl.multiple_of(256 * x + LANES, LANES)
        rows = total_ref[pl.ds(first, 256), :]
        low = dproj_ref[:, pl.ds(first, LANES)]
        high = dproj_ref[:, pl.ds(second, LANES)]
        cross = rows[:, :LANES] + rows[:, LANES:]
        for n, part in enumerate((low, high)):
            turned = jnp.concatenate([jnp.zeros((96, LANES), F32), part[0:32]], axis=0).T
            out_ref[LANES * n : LANES * (n + 1), :] = jnp.where(
                lane_ids((LANES, LANES)) >= 96, turned, cross[LANES * n : LANES * (n + 1)]
            )
        out_ref[256:288, :] = low[32:64]
        out_ref[288:320, :] = high[32:64]
        dose_own = []
        for z in range(8):
            row = (low, high)[z // 4][64:65]
            dose_own.append(pltpu.roll(row, 96 - 32 * (z % 4), 1) if z % 4 < 3 else row)
        pieces = jnp.concatenate(own + dose_own + [jnp.zeros((53, LANES), F32)], axis=0)
        out_ref[320:384, :] = jnp.where(spare, pieces, proj)


def cross_products(bin_ids, table, dosages, covariates, plates, dose_proj):
    count, width = dosages.shape
    chunk = CROSS_CHUNK
    steps = width // chunk
    whole = pl.BlockSpec(memory_space=pltpu.VMEM)
    hbm = pl.BlockSpec(memory_space=pl.ANY)
    return pl.pallas_call(
        cross_kernel,
        in_specs=[hbm, whole, hbm, hbm, hbm, whole],
        out_specs=[whole] * 4,
        out_shape=[jax.ShapeDtypeStruct((384, LANES), F32)] * 4,
        scratch_shapes=[
            pltpu.VMEM((steps, bin_ids.shape[0], chunk), jnp.int32),
            pltpu.VMEM((COVARS, width), F32),
            pltpu.VMEM((1, width), jnp.int32),
            pltpu.VMEM((steps, count, chunk), BF16),
            pltpu.VMEM((steps, 256, chunk), BF16),
            pltpu.VMEM((count, 256), F32),
            pltpu.VMEM((192, 256), F32),
            pltpu.VMEM((LANES, LANES), F32),
            pltpu.SemaphoreType.DMA((2 * steps + 2,)),
        ],
        compiler_params=vmem_params(50),
        name="cross_products",
    )(bin_ids, table, dosages, covariates, plates, dose_proj)


def regroup_kernel(own_ref, first_ref, second_ref, third_ref, out_ref):
    total = own_ref[...] + first_ref[...] + second_ref[...] + third_ref[...]
    proj = total[320:384]
    halves = [
        jnp.concatenate(
            [total[LANES * n : LANES * (n + 1)].T[96:128], total[256 + 32 * n : 288 + 32 * n]],
            axis=0,
        )
        for n in range(2)
    ]
    for z in range(8):
        squares = jnp.concatenate(
            [proj[0:3], proj[3 + z : 4 + z], jnp.zeros((28, LANES), F32)], axis=0
        )
        cross = total[32 * z : 32 * z + 32]
        out_ref[z, 0:32, :] = jnp.where(lane_ids((32, LANES)) >= 96, squares, cross)
        dose = halves[z // 4]
        dose = pltpu.roll(dose, 96 - 32 * (z % 4), 1) if z % 4 < 3 else dose
        out_ref[z, 32:96, :] = jnp.where(lane_ids((64, LANES)) >= 96, dose, proj)


def regroup(*parts):
    whole = pl.BlockSpec(memory_space=pltpu.VMEM)
    return pl.pallas_call(
        regroup_kernel,
        in_specs=[whole] * 4,
        out_specs=whole,
        out_shape=jax.ShapeDtypeStruct((8, 96, LANES), F32),
        compiler_params=vmem_params(8),
        name="regroup",
    )(*parts)


def inverse_kernel(gram_ref, out_ref):
    packed = gram_ref[...]
    lane = lane_ids((DESIGN, LANES))
    row = lax.broadcasted_iota(jnp.int32, (DESIGN, LANES), 0)
    work = jnp.concatenate([packed, pltpu.roll(packed, 64, 1)], axis=0)
    work = jnp.where(lane < DESIGN, work, jnp.where(lane == row + DESIGN, 1.0, 0.0))
    plate = work[COVARS:]
    low_lane = lane_ids((PLATES, LANES))
    low_row = lax.broadcasted_iota(jnp.int32, (PLATES, LANES), 0)
    pivots = jnp.sum(
        jnp.where(low_lane == low_row + COVARS, plate, 0.0), axis=1, keepdims=True
    )
    upper = work[:COVARS]
    coupling = upper[:, COVARS:DESIGN]
    upper = upper - lax.dot_general(
        coupling, plate * (1.0 / pivots), NN, precision=exact_mode, preferred_element_type=F32
    )
    for k in range(COVARS):
        first = k // 8 * 8
        source = upper[k : k + 1]
        rest = upper[first:]
        scale = 1.0 / source[:, k : k + 1]
        below = lax.broadcasted_iota(jnp.int32, rest.shape, 0) > k - first
        factor = jnp.where(below, rest[:, k : k + 1] * (source * scale), 0.0)
        rest = rest - factor
        upper = jnp.concatenate([upper[:first], rest], axis=0) if first else rest
    work = jnp.concatenate([upper, plate], axis=0)
    diagonal = jnp.sum(jnp.where(lane == row, work, 0.0), axis=1, keepdims=True)
    out_ref[...] = pltpu.roll(work * lax.rsqrt(diagonal), 64, 1)[:, :DESIGN]


def inverse_factor(table):
    return pl.pallas_call(
        inverse_kernel,
        grid=(1,),
        in_specs=[pl.BlockSpec((32, LANES), lambda i: (23, 0))],
        out_specs=pl.BlockSpec((DESIGN, DESIGN), lambda i: (0, 0)),
        out_shape=jax.ShapeDtypeStruct((DESIGN, DESIGN), F32),
        compiler_params=vmem_params(8),
        cost_estimate=pl.CostEstimate(flops=4_000_000_000, bytes_accessed=32768, transcendentals=0),
        name="inverse_factor",
    )(table)


def finish_kernel(freedom, parts_ref, inverse_ref, out_ref):
    total = parts_ref[0]
    for z in range(1, 8):
        total = total + parts_ref[z]
    shape = (32, LANES)
    lane = lane_ids((1, LANES))
    white = lax.dot_general(
        inverse_ref[...], total[32:96], NN, precision=exact_mode, preferred_element_type=F32
    )
    shared = lax.dot_general(
        white, white, (((0,), (0,)), ((), ())), precision=exact_mode, preferred_element_type=F32
    )
    removed = jnp.sum(white * white, axis=0, keepdims=True)
    expr_sq = [pltpu.roll(total[j : j + 1], 32 * j + 32, 1) for j in range(3)]
    expr_sq = jnp.where(lane < 32, expr_sq[0], jnp.where(lane < 64, expr_sq[1], expr_sq[2]))
    expr_norm = expr_sq - removed
    own = lane_ids(shape) == lax.broadcasted_iota(jnp.int32, shape, 0) + 96
    dose_norm = jnp.broadcast_to(total[3:4] - removed, shape)
    dose_norm = jnp.sum(jnp.where(own, dose_norm, 0.0), axis=1, keepdims=True)
    cross = total[0:32] - shared[96:128]
    corr = cross * lax.rsqrt(dose_norm * expr_norm + tiny_eps)
    stats = corr * jnp.sqrt(freedom / (1.0 - corr * corr))
    out_ref[...] = stats[:, : out_ref.shape[1]]


def finish(parts, inverse, freedom, proteins):
    whole = pl.BlockSpec(memory_space=pltpu.VMEM)
    return pl.pallas_call(
        functools.partial(finish_kernel, float(freedom)),
        in_specs=[whole, whole],
        out_specs=whole,
        out_shape=jax.ShapeDtypeStruct((32, proteins), F32),
        compiler_params=vmem_params(8),
        name="finish",
    )(parts, inverse)


def body(bin_ids, plate_ids, covariates, dosages):
    sample_total = bin_ids.shape[1] * lax.axis_size("samp")
    plates = plate_ids[None, :]
    z_groups = [[x * 8 + z for z in range(8)] for x in range(4)]

    counts = histogram(bin_ids, covariates, plates).reshape(32, 24, LANES)
    counts = lax.all_to_all(counts, "samp", 0, 0, tiled=True)
    dose_proj = dose_products(dosages, covariates, plates)
    counts, dose_proj = lax.optimization_barrier((counts, dose_proj))
    table = rank_table(counts, sample_total)
    table = lax.all_to_all(table, "samp", 0, 0, tiled=True).reshape(768, LANES)
    own, *others = cross_products(
        bin_ids, table, dosages, covariates, plates, dose_proj
    )
    late_table, own = lax.optimization_barrier((table, own))
    inverse = inverse_factor(late_table)
    moved = {}
    for d in (2, 1, 3):
        pairs = [(x * 8 + z, (x + d) % 4 * 8 + z) for x in range(4) for z in range(8)]
        moved[d] = lax.ppermute(others[d - 1], "samp", pairs)
    own, inverse = lax.optimization_barrier((own, inverse))
    parts = regroup(own, moved[1], moved[2], moved[3])
    parts = lax.all_to_all(parts, "samp", 0, 0, axis_index_groups=z_groups, tiled=True)
    return finish(parts, inverse, sample_total - DESIGN - 1.0, bin_ids.shape[0])


def solution(mesh):
    placed = (P("prot", "samp"), P("samp"), P(None, "samp"), P(None, "samp"))
    return jax.shard_map(
        body, mesh=mesh, in_specs=placed, out_specs=P("samp", "prot"), check_vma=False
    )
```
